512 devices in a mesh: dp: 64 (over z, y), tensor: 8 (over x, core).
Axes of the slice: x: 4, y: 8, z: 8, core: 2. Of those that a mesh axis runs over, the one named last changes fastest.
Arguments:
- queries: bfloat16 [4096, 8, 8192], P('dp', None, 'tensor'), may hold values from -150 to 150
- text_kv: bfloat16 [4096, 8, 2048], P('dp', None, 'tensor'), may hold values from -7 to 7
- visual_kv: bfloat16 [256, 64, 2048], P('dp', None, 'tensor'), may hold values from -6 to 6
- loss_gain: float32 [8192], P('tensor'), may hold values from 0.5 to 4.5
- response_image: int32 [4096], replicated, may hold values from 0 to 255, as said below
- visual_rows: int32 [256], replicated, may hold values from 1 to 64, as said below
- text_length: int32 [4096], replicated, may hold values from 1 to 8, as said below
Outputs:
- visual_grad: bfloat16 [256, 64, 2048], P('dp', None, 'tensor')
- text_grad: bfloat16 [4096, 8, 2048], P('dp', None, 'tensor')
- loss: float32 [4096], P('dp')
The draws below stay inside these ranges and needn't reach their ends.
Inputs may be any that keep to these rules, and one draw needn't show every extreme that they name: For each d, the responses d * 64 to d * 64 + 63 have images of every index of dp once each: response_image[r] // 4 takes each value 0 to 63 once among them. Every image has exactly 16 responses. `visual_rows`: some image uses all 64 rows. `text_length`: some response uses all 8 tokens.
All inputs are finite; a program needn't handle non-finite values.
Results may differ from the reference program's by a relative error of at most 0.04.
Values may be sent and summed in bfloat16 or wider, within the bound.
A program may use at most 64 MiB of HBM per device.

```python
import math
import jax
import jax.numpy as jnp
from jax import lax

HEADS = 64
KV_HEADS = 8
HD = 128
GROUP = 16
TXT = 8
VIS = 64
IMG_DEV = 4
IMAGES = 256
RESPONSES = 4096
N_DP = 64


def text_parts(key, lift_size):
    query_seed, key_seed, value_seed, mark_seed, power_seed, jitter_seed = jax.random.split(key, 6)
    heads_per = HEADS // KV_HEADS
    key_rows = jnp.clip(jax.random.normal(key_seed, (RESPONSES, TXT, KV_HEADS, HD), jnp.float32), -6.0, 6.0)
    value_rows = jnp.clip(jax.random.normal(value_seed, (RESPONSES, TXT, KV_HEADS, HD), jnp.float32), -6.0, 6.0)
    query_rows = jnp.clip(jax.random.normal(query_seed, (RESPONSES, TXT, KV_HEADS, heads_per, HD), jnp.float32), -6.0, 6.0)
    chosen = jax.random.randint(mark_seed, (RESPONSES, TXT, KV_HEADS), 0, 12) == 0
    even_spot = (jnp.arange(TXT) % 2 == 0) & (jnp.arange(TXT) >= 2)
    chosen = chosen & even_spot[None, :, None] & (lift_size > 0.0)
    strength = (10 + 7 * jax.random.randint(power_seed, (RESPONSES, TXT, KV_HEADS), 0, 3)).astype(jnp.float32) * lift_size
    earlier = jnp.roll(key_rows, 1, axis=1)
    jitter = jnp.clip(jax.random.normal(jitter_seed, key_rows.shape, jnp.float32), -6.0, 6.0)
    key_rows = jnp.where(chosen[..., None], earlier + 0.1 * jitter, key_rows)
    query_rows = jnp.where(chosen[..., None, None], strength[..., None, None] * earlier[:, :, :, None, :], query_rows)
    return (query_rows, key_rows, value_rows)


def draw_queries(key, part):
    query_rows, key_rows, value_rows = text_parts(key, 0.0)
    return query_rows.reshape(RESPONSES, TXT, HEADS * HD).astype(jnp.bfloat16)


def draw_text_kv(key, part):
    query_rows, key_rows, value_rows = text_parts(key, 0.0)
    stacked = jnp.stack([key_rows, value_rows], axis=3)
    return stacked.reshape(RESPONSES, TXT, 2 * KV_HEADS * HD).astype(jnp.bfloat16)


def draw_loss_gain(key, part):
    key = jax.random.fold_in(key, 17)
    width_all = HEADS * HD
    log_spread = jax.random.uniform(key, (width_all,), jnp.float32, math.log(0.5), math.log(1.5))
    rising = 3.0 ** (jnp.arange(width_all, dtype=jnp.float32) / (width_all - 1))
    return jnp.exp(log_spread) * rising


def draw_response_image(key, part):
    key = jax.random.fold_in(key, 11)
    owner_key, slot_key = jax.random.split(key)
    owner_seeds = jax.random.split(owner_key, N_DP)
    slot_seeds = jax.random.split(slot_key, N_DP)
    orders = jax.vmap(lambda one_seed: jax.random.permutation(one_seed, N_DP))(owner_seeds)
    owner_table = jnp.arange(N_DP, dtype=jnp.int32)[:, None] * IMG_DEV + orders.astype(jnp.int32) // GROUP
    holder_table = owner_table.T
    slot_owner = jax.vmap(lambda one_seed: jax.random.permutation(one_seed, N_DP))(slot_seeds).astype(jnp.int32)
    placed = jnp.take_along_axis(holder_table, slot_owner, axis=1)
    return placed.reshape(-1).astype(jnp.int32)


def draw_visual_rows(key, part):
    key = jax.random.fold_in(key, 23)
    count_seed, spot_seed = jax.random.split(key)
    counts = jax.random.randint(count_seed, (IMAGES,), 1, VIS + 1)
    spot = jax.random.randint(spot_seed, (), 0, IMAGES)
    return counts.at[spot].set(VIS).astype(jnp.int32)


def draw_text_length(key, part):
    key = jax.random.fold_in(key, 29)
    count_seed, spot_seed = jax.random.split(key)
    counts = jax.random.randint(count_seed, (RESPONSES,), 1, TXT + 1)
    spot = jax.random.randint(spot_seed, (), 0, RESPONSES)
    return counts.at[spot].set(TXT).astype(jnp.int32)


def block_levels(own_key, extent, shards, smallest, top_value):
    loudness, own = 1.0, jax.random.fold_in(own_key, 6)
    for dim, shards_of in shards:
        steps = jnp.exp(jax.random.uniform(jax.random.fold_in(own, dim), (shards_of,), jnp.float32, smallest / len(shards), top_value / len(shards)))
        loudness = loudness * jnp.repeat(steps, extent[dim] // shards_of).reshape([-1 if axis == dim else 1 for axis in range(len(extent))])
    return loudness


def bell_draw(rng, dims, width, most, pieces=(), kind=jnp.bfloat16):
    values = jax.random.normal(rng, dims, jnp.float32) * width
    if len(pieces) > 0:
        values = block_levels(rng, dims, pieces, -0.22, 0.18) * values
    return jnp.clip(values, min=-most, max=most).astype(kind)


def setup_inputs(seed: int = 0) -> dict:
    key_of = jax.random.split(jax.random.key(seed), 8)
    return {
        "queries": draw_queries(jax.random.fold_in(key_of[7], 71), 0),
        "text_kv": draw_text_kv(jax.random.fold_in(key_of[7], 71), 0),
        "visual_kv": bell_draw(key_of[2], (IMAGES, VIS, 2 * KV_HEADS * HD), 1.0, 6.0, ((0, 64), (2, 8))),
        "loss_gain": draw_loss_gain(jax.random.fold_in(key_of[7], 71), 0),
        "response_image": draw_response_image(jax.random.fold_in(key_of[7], 71), 0),
        "visual_rows": draw_visual_rows(jax.random.fold_in(key_of[7], 71), 0),
        "text_length": draw_text_length(jax.random.fold_in(key_of[7], 71), 0),
    }


def multiply(form, left, right):
    return jnp.einsum(form, left.astype(jnp.float32), right.astype(jnp.float32))


def attend(queries, text_kv, image_kv, seen_rows, length, loss_gain):
    resp_count, text_steps, query_width = queries.shape
    kv_heads = text_kv.shape[-1] // (2 * HD)
    groups = query_width // (HD * kv_heads)
    vis_rows = image_kv.shape[1]
    all_rows = vis_rows + text_steps
    query_heads = queries.reshape(resp_count, text_steps, kv_heads, groups, HD)
    key_value = jnp.concatenate([image_kv, text_kv], axis=1).reshape(resp_count, all_rows, kv_heads, 2, HD)
    key_rows = key_value[:, :, :, 0]
    value_rows = key_value[:, :, :, 1]
    scores = multiply('jtkgd,jskd->jkgts', query_heads, key_rows) * HD ** -0.5
    key_index = jnp.arange(all_rows, dtype=jnp.int32)
    query_index = jnp.arange(text_steps, dtype=jnp.int32)
    vis_allowed = key_index[None, None, :] < seen_rows[:, None, None]
    text_index = key_index - vis_rows
    text_allowed = (key_index[None, None, :] >= vis_rows) & (text_index[None, None, :] <= query_index[None, :, None]) & (text_index[None, None, :] < length[:, None, None])
    allowed = vis_allowed | text_allowed
    scores = jnp.where(allowed[:, None, None], scores, jnp.float32(-1e30))
    row_max = jnp.max(scores, axis=-1, keepdims=True)
    raw_weights = jnp.exp(scores - row_max)
    prob = raw_weights / jnp.sum(raw_weights, axis=-1, keepdims=True)
    prob_bf = prob.astype(jnp.bfloat16)
    attended = multiply('jkgts,jskd->jtkgd', prob_bf, value_rows)
    flat_out = attended.reshape(resp_count, text_steps, query_width)
    live_mask = (query_index[None, :] < length[:, None]).astype(jnp.float32)
    loss_part = jnp.sum(live_mask[:, :, None] * loss_gain[None, None, :] * flat_out * flat_out, axis=(1, 2)) / (2.0 * text_steps * HD)
    cotangent = (live_mask[:, :, None] * loss_gain[None, None, :] * flat_out).astype(jnp.bfloat16)
    cot_heads = cotangent.reshape(resp_count, text_steps, kv_heads, groups, HD)
    value_grad = multiply('jkgts,jtkgd->jskd', prob_bf, cot_heads)
    prob_grad = multiply('jtkgd,jskd->jkgts', cot_heads, value_rows)
    row_delta = jnp.transpose(jnp.sum(cot_heads.astype(jnp.float32) * attended, axis=-1), (0, 2, 3, 1))
    score_grad = (prob * (prob_grad - row_delta[..., None])).astype(jnp.bfloat16)
    key_grad = multiply('jkgts,jtkgd->jskd', score_grad, query_heads) * HD ** -0.5
    all_grads = jnp.stack([key_grad, value_grad], axis=3).reshape(resp_count, all_rows, 2 * kv_heads * HD)
    return loss_part, all_grads[:, :vis_rows], all_grads[:, vis_rows:]


def reference(queries, text_kv, visual_kv, loss_gain, response_image, visual_rows, text_length):
    blocks = RESPONSES // N_DP
    query_width = queries.shape[-1]
    kv_width = text_kv.shape[-1]
    query_blocks = queries.reshape(blocks, N_DP, TXT, query_width)
    text_blocks = text_kv.reshape(blocks, N_DP, TXT, kv_width)
    block_ids = response_image.reshape(blocks, N_DP).astype(jnp.int32)
    block_lengths = text_length.reshape(blocks, N_DP).astype(jnp.int32)

    def scan_step(accumulated, block_item):
        query_part, text_part, id_part, length_part = block_item
        image_rows = jnp.take(visual_kv, id_part, axis=0)
        seen_rows = jnp.take(visual_rows, id_part).astype(jnp.int32)
        loss_part, vis_grad, txt_grad = attend(query_part, text_part, image_rows, seen_rows, length_part, loss_gain)
        rounded = lax.optimization_barrier(vis_grad.astype(jnp.bfloat16))
        accumulated = accumulated.at[id_part].add(rounded.astype(jnp.float32))
        return accumulated, (loss_part, txt_grad.astype(jnp.bfloat16))

    start = jnp.zeros(visual_kv.shape, jnp.float32)
    summed, (loss_pieces, text_pieces) = lax.scan(scan_step, start, (query_blocks, text_blocks, block_ids, block_lengths))
    visual_grad = summed.astype(jnp.bfloat16)
    text_grad = text_pieces.reshape(RESPONSES, TXT, kv_width)
    loss = loss_pieces.reshape(RESPONSES)
    return visual_grad, text_grad, loss
```

```python
import functools

import jax
import jax.numpy as jnp
from jax import lax
from jax.experimental import pallas as pl
from jax.experimental.pallas import tpu as pltpu
from jax.sharding import PartitionSpec as P

HD = 128
MESH = pl.DeviceIdType.MESH
SIDE = 8
N_DP = 64
TENSOR = 8
VIS = 64
TXT = 8
HEADS = 8
ROWS = HEADS * TXT
BLOCK = ROWS + 2 * TXT
KEYS = VIS + 2 * TXT
CHUNK = 8
SLOTS = N_DP
SCALE = HD ** (-0.5)

NT = (((1,), (1,)), ((), ()))
NN = (((1,), (0,)), ((), ()))
TN = (((0,), (0,)), ((), ()))


def dot(left, right, dims):
    return lax.dot_general(left, right, dims, preferred_element_type=jnp.float32)


def offset(group, turn):
    a, b = 1 + group % 4, 3 - group // 4
    last = group // 15
    if turn == 0:
        return a, b
    if turn == 1:
        return b, -a
    if turn == 2:
        return -a, -b + 4 * last
    return -b, a - 4 * last


def kernel(
    meta, rows4, q_ref, text_ref, kv_ref, gain_ref, place_ref,
    vis_out, text_out, loss_out,
    send_buf, recv_buf, key4, val4, acc, back_send, back_recv, loss_send, loss_recv, loss_parts,
    send_sem, recv_sem, back_send_sem, back_recv_sem, loss_send_sem, loss_recv_sem, part_send_sem, part_recv_sem,
):
    me = lax.axis_index("dp")
    core = lax.axis_index("tensor")
    z, y = me // SIDE, me % SIDE

    def target(group, turn):
        dz, dy = offset(group, turn)
        return ((z + dz + SIDE) % SIDE) * SIDE + (y + dy + SIDE) % SIDE

    def origin(group, turn):
        dz, dy = offset(group, turn)
        return ((z - dz + SIDE) % SIDE) * SIDE + (y - dy + SIDE) % SIDE

    barrier = pltpu.get_barrier_semaphore()

    def greet(step, carry):
        peer = (me + step) % N_DP
        pl.semaphore_signal(barrier, inc=1, device_id=(peer, core), device_id_type=MESH)
        return carry

    lax.fori_loop(1, N_DP, greet, 0)
    for step in range(1, TENSOR):
        pl.semaphore_signal(barrier, inc=1, device_id=(me, (core + step) % TENSOR), device_id_type=MESH)

    for image in range(4):
        key4[image] = kv_ref[image, :, 0:HD]
        val4[image] = kv_ref[image, :, HD : 2 * HD]
    acc[...] = jnp.zeros_like(acc)
    pl.semaphore_wait(barrier, N_DP - 1 + TENSOR - 1)

    def stage(slot, peer, where):
        response = meta[0, peer]
        wide = q_ref[response].astype(jnp.float32)
        stacked = jnp.concatenate([wide[:, h * HD : (h + 1) * HD] for h in range(HEADS)], axis=0)
        where[slot, 0:ROWS] = stacked.astype(jnp.bfloat16)
        text = text_ref[response].astype(jnp.float32)
        pair = jnp.concatenate([text[:, 0:HD], text[:, HD : 2 * HD]], axis=0)
        where[slot, ROWS:BLOCK] = pair.astype(jnp.bfloat16)

    def send(slot, peer):
        pltpu.make_async_remote_copy(
            src_ref=send_buf.at[slot],
            dst_ref=recv_buf.at[slot],
            send_sem=send_sem.at[slot // CHUNK],
            recv_sem=recv_sem.at[slot // CHUNK],
            device_id=(peer, core),
            device_id_type=MESH,
        ).start()

    def dispatch(group, carry):
        for turn in range(4):
            slot, peer = 4 * group + turn, target(group, turn)
            stage(slot, peer, send_buf)
            send(slot, peer)
        return carry

    lax.fori_loop(0, 15, dispatch, 0)
    for turn in range(3):
        stage(60 + turn, target(15, turn), send_buf)
        send(60 + turn, target(15, turn))
    stage(63, me, recv_buf)

    lane = lax.broadcasted_iota(jnp.int32, (1, HD), 1)
    first = lane < ROWS
    step_of = lane % TXT
    row = lax.broadcasted_iota(jnp.int32, (VIS + TXT, HD), 0)
    gain_t = gain_ref[...]

    def key_rows(both):
        return jnp.where(first, both[0 : VIS + TXT], both[KEYS : KEYS + VIS + TXT])

    def value_rows(both):
        both = [jnp.concatenate([both[b : b + VIS], both[b + VIS + TXT : b + KEYS]], axis=0) for b in (0, KEYS)]
        return jnp.where(first, both[0], both[1])

    none = jnp.zeros((TXT, HD), jnp.float32)

    def diagonal(parts):
        values = jnp.concatenate(parts, axis=0)
        zero = jnp.zeros_like(values)
        return jnp.concatenate([jnp.where(first, values, zero), jnp.where(first, zero, values)], axis=0).astype(
            jnp.bfloat16
        )

    def work(slot, peers):
        images = [meta[1, peer] for peer in peers]
        lengths = [meta[2, peer] for peer in peers]
        seen = [rows4[image] for image in images]
        blocks = [recv_buf[slot + i] for i in range(2)]
        texts = [block[ROWS:BLOCK] for block in blocks]
        queries = jnp.concatenate([block[0:ROWS] for block in blocks], axis=0)
        keys = jnp.concatenate([key4[images[0]], texts[0], key4[images[1]], texts[1]], axis=0)
        values = jnp.concatenate([val4[images[0]], texts[0], val4[images[1]], texts[1]], axis=0)
        length = jnp.where(first, lengths[0], lengths[1])
        visible = jnp.where(first, seen[0], seen[1])
        text_end = VIS + jnp.minimum(step_of + 1, length)
        allowed = (row < visible) | ((row >= VIS) & (row < text_end))
        scores = jnp.where(allowed, key_rows(dot(keys, queries, NT)) * SCALE, jnp.float32(-1e30))
        raw = jnp.exp(scores - jnp.max(scores, axis=0, keepdims=True))
        prob = raw * (1.0 / jnp.sum(raw, axis=0, keepdims=True))
        prob2 = diagonal([prob[0:VIS], none, prob[VIS:]])
        attended = dot(values, prob2, TN)
        live = (step_of < length).astype(jnp.float32)
        weighted = gain_t * attended * live
        loss_row = jnp.sum(weighted * attended, axis=0, keepdims=True) * (1.0 / (2.0 * TXT * HD))
        cot = weighted.astype(jnp.bfloat16)
        delta = jnp.sum(cot.astype(jnp.float32) * attended, axis=0, keepdims=True)
        prob_grad = value_rows(dot(values, cot, NN))
        score_grad2 = diagonal([prob * (prob_grad - delta), none])
        value_grad = dot(prob2, cot, NT)
        key_grad = dot(score_grad2, queries, NN) * SCALE
        zero = jnp.zeros_like(loss_row)
        losses = [jnp.where(first, loss_row, zero), jnp.where(first, zero, loss_row)]
        backs, visuals = [], []
        for i in range(2):
            base = i * KEYS
            backs.append(
                jnp.concatenate(
                    [key_grad[base + VIS : base + VIS + TXT], value_grad[base + VIS + TXT : base + KEYS]], axis=0
                ).astype(jnp.bfloat16)
            )
            visuals.append(
                jnp.concatenate([key_grad[base : base + VIS], value_grad[base : base + VIS]], axis=0)
                .astype(jnp.bfloat16)
                .astype(jnp.float32)
            )
        for image in range(4):
            acc[image] += jnp.where(images[0] == image, visuals[0], 0.0) + jnp.where(
                images[1] == image, visuals[1], 0.0
            )
        return backs, losses

    def back(slot, peer):
        pltpu.make_async_remote_copy(
            src_ref=back_send.at[slot],
            dst_ref=back_recv.at[slot],
            send_sem=back_send_sem.at[0],
            recv_sem=back_recv_sem.at[0],
            device_id=(peer, core),
            device_id_type=MESH,
        ).start()
        pltpu.make_async_remote_copy(
            src_ref=loss_send.at[pl.ds(slot, 1)],
            dst_ref=loss_recv.at[pl.ds(slot, 1)],
            send_sem=loss_send_sem.at[0],
            recv_sem=loss_recv_sem.at[0],
            device_id=(peer, core),
            device_id_type=MESH,
        ).start()

    def arrived(first_slot, count, chunk):
        pltpu.make_async_remote_copy(
            src_ref=send_buf.at[pl.ds(first_slot, count)],
            dst_ref=recv_buf.at[pl.ds(first_slot, count)],
            send_sem=send_sem.at[chunk],
            recv_sem=recv_sem.at[chunk],
            device_id=(me, core),
            device_id_type=MESH,
        ).wait_recv()

    def chunk_step(chunk, carry):
        arrived(chunk * CHUNK, CHUNK, chunk)
        for pair in range(CHUNK // 2):
            group, turn = 2 * chunk + pair // 2, 2 * (pair % 2)
            slot = 4 * group + turn
            peers = [origin(group, turn + i) for i in range(2)]
            backs, losses = work(slot, peers)
            for i in range(2):
                back_send[slot + i] = backs[i]
                loss_send[pl.ds(slot + i, 1)] = losses[i]
                back(slot + i, peers[i])
        return carry

    lax.fori_loop(0, 7, chunk_step, 0)
    arrived(56, 7, 7)
    for pair in range(CHUNK // 2):
        group, turn = 14 + pair // 2, 2 * (pair % 2)
        slot = 4 * group + turn
        peers = [origin(group, turn + i) for i in range(2)]
        backs, losses = work(slot, peers)
        for i in range(2):
            if slot + i < SLOTS - 1:
                back_send[slot + i] = backs[i]
                loss_send[pl.ds(slot + i, 1)] = losses[i]
                back(slot + i, peers[i])
            else:
                back_recv[slot + i] = backs[i]
                loss_recv[pl.ds(slot + i, 1)] = losses[i]

    for image in range(4):
        total = acc[image]
        vis_out[image] = jnp.concatenate([total[0:VIS], total[VIS : 2 * VIS]], axis=1).astype(jnp.bfloat16)

    remote = SLOTS - 1
    losses_in = pltpu.make_async_remote_copy(
        src_ref=loss_send.at[pl.ds(0, remote)],
        dst_ref=loss_recv.at[pl.ds(0, remote)],
        send_sem=loss_send_sem.at[0],
        recv_sem=loss_recv_sem.at[0],
        device_id=(me, core),
        device_id_type=MESH,
    )
    losses_in.wait_recv()
    per_slot = jnp.sum(loss_recv[...], axis=1, keepdims=True)
    slot_id = lax.broadcasted_iota(jnp.int32, (SLOTS, HD), 0)
    mine = jnp.sum(jnp.where(slot_id == place_ref[...], per_slot, 0.0), axis=0, keepdims=True)
    loss_parts[core] = mine
    for step in range(1, TENSOR):
        pltpu.make_async_remote_copy(
            src_ref=loss_parts.at[core],
            dst_ref=loss_parts.at[core],
            send_sem=part_send_sem.at[step],
            recv_sem=part_recv_sem.at[step],
            device_id=(me, (core + step) % TENSOR),
            device_id_type=MESH,
        ).start()

    backs_in = pltpu.make_async_remote_copy(
        src_ref=back_send.at[pl.ds(0, remote)],
        dst_ref=back_recv.at[pl.ds(0, remote)],
        send_sem=back_send_sem.at[0],
        recv_sem=back_recv_sem.at[0],
        device_id=(me, core),
        device_id_type=MESH,
    )
    backs_in.wait_recv()

    def place(response, carry):
        block = back_recv[meta[3, response]].astype(jnp.float32)
        text_out[response] = jnp.concatenate([block[0:TXT], block[TXT : 2 * TXT]], axis=1).astype(jnp.bfloat16)
        return carry

    lax.fori_loop(0, N_DP, place, 0, unroll=8)

    total = mine
    for step in range(1, TENSOR):
        peer = (core + TENSOR - step) % TENSOR
        pltpu.make_async_remote_copy(
            src_ref=loss_parts.at[peer],
            dst_ref=loss_parts.at[peer],
            send_sem=part_send_sem.at[step],
            recv_sem=part_recv_sem.at[step],
            device_id=(me, core),
            device_id_type=MESH,
        ).wait()
        total = total + loss_parts[peer]
    loss_out[...] = total

    losses_in.wait_send()
    backs_in.wait_send()
    for chunk in range(SLOTS // CHUNK):
        count = CHUNK if chunk < 7 else CHUNK - 1
        pltpu.make_async_remote_copy(
            src_ref=send_buf.at[pl.ds(chunk * CHUNK, count)],
            dst_ref=recv_buf.at[pl.ds(chunk * CHUNK, count)],
            send_sem=send_sem.at[chunk],
            recv_sem=recv_sem.at[chunk],
            device_id=(me, core),
            device_id_type=MESH,
        ).wait_send()


def local(queries, text_kv, visual_kv, loss_gain, response_image, visual_rows, text_length):
    me = lax.axis_index("dp")
    owned = visual_kv.shape[0]
    image_table = response_image.reshape(N_DP, N_DP)
    length_table = text_length.reshape(N_DP, N_DP)
    positions = jnp.arange(N_DP, dtype=jnp.int32)
    held = image_table // owned == me
    slot_image = jnp.sum(jnp.where(held, image_table % owned, 0), axis=1)
    slot_length = jnp.sum(jnp.where(held, length_table, 0), axis=1)
    owner = lax.dynamic_index_in_dim(image_table, me, 0, keepdims=False) // owned
    response_of = jnp.sum(jnp.where(owner[None, :] == positions[:, None], positions[None, :], 0), axis=1)
    dz = (owner // SIDE - me // SIDE + SIDE) % SIDE
    dy = (owner % SIDE - me % SIDE + SIDE) % SIDE
    slot_table = [0] * N_DP
    for group in range(16):
        for turn in range(4):
            a, b = offset(group, turn)
            slot_table[(a % SIDE) * SIDE + b % SIDE] = 4 * group + turn
    slot_of_offset = jnp.array(slot_table, dtype=jnp.int32)
    offset_id = dz * SIDE + dy
    place = jnp.sum(jnp.where(offset_id[:, None] == positions[None, :], slot_of_offset[None, :], 0), axis=1)
    meta = jnp.stack([response_of, slot_image, slot_length, place])
    rows4 = lax.dynamic_slice_in_dim(visual_rows, me * owned, owned)
    place_row = jnp.concatenate([place, jnp.full((HD - N_DP,), -1, jnp.int32)])[None, :]
    gain = loss_gain.reshape(HEADS, HD).T
    gain_t = jnp.tile(jnp.repeat(gain, TXT, axis=1), (1, 2))
    vmem = pl.BlockSpec(memory_space=pltpu.VMEM)
    smem = pl.BlockSpec(memory_space=pltpu.SMEM)
    vis_grad, text_grad, loss = pl.pallas_call(
        kernel,
        out_shape=(
            jax.ShapeDtypeStruct(visual_kv.shape, jnp.bfloat16),
            jax.ShapeDtypeStruct(text_kv.shape, jnp.bfloat16),
            jax.ShapeDtypeStruct((1, HD), jnp.float32),
        ),
        in_specs=[smem, smem] + [vmem] * 5,
        out_specs=[vmem] * 3,
        scratch_shapes=[
            pltpu.VMEM((SLOTS, BLOCK, HD), jnp.bfloat16),
            pltpu.VMEM((SLOTS, BLOCK, HD), jnp.bfloat16),
            pltpu.VMEM((4, VIS, HD), jnp.bfloat16),
            pltpu.VMEM((4, VIS, HD), jnp.bfloat16),
            pltpu.VMEM((4, 2 * VIS, HD), jnp.float32),
            pltpu.VMEM((SLOTS, 2 * TXT, HD), jnp.bfloat16),
            pltpu.VMEM((SLOTS, 2 * TXT, HD), jnp.bfloat16),
            pltpu.VMEM((SLOTS, HD), jnp.float32),
            pltpu.VMEM((SLOTS, HD), jnp.float32),
            pltpu.VMEM((TENSOR, 1, HD), jnp.float32),
            pltpu.SemaphoreType.DMA((8,)),
            pltpu.SemaphoreType.DMA((8,)),
            pltpu.SemaphoreType.DMA((1,)),
            pltpu.SemaphoreType.DMA((1,)),
            pltpu.SemaphoreType.DMA((1,)),
            pltpu.SemaphoreType.DMA((1,)),
            pltpu.SemaphoreType.DMA((TENSOR,)),
            pltpu.SemaphoreType.DMA((TENSOR,)),
        ],
        compiler_params=pltpu.CompilerParams(
            collective_id=0, has_side_effects=True, vmem_limit_bytes=32 * 1024 * 1024
        ),
        cost_estimate=pl.CostEstimate(flops=400_000_000, bytes_accessed=2_000_000, transcendentals=300_000),
    )(meta, rows4, queries, text_kv, visual_kv, gain_t, place_row)
    return vis_grad, text_grad, loss[0, :N_DP]


def solution(mesh):
    in_specs = (
        P("dp", None, "tensor"),
        P("dp", None, "tensor"),
        P("dp", None, "tensor"),
        P("tensor"),
        P(),
        P(),
        P(),
    )
    out_specs = (P("dp", None, "tensor"), P("dp", None, "tensor"), P("dp"))
    return jax.shard_map(local, mesh=mesh, in_specs=in_specs, out_specs=out_specs, check_vma=False)
```

```python
import functools

import jax
import jax.numpy as jnp
from jax import lax
from jax.experimental import pallas as pl
from jax.experimental.pallas import tpu as pltpu
from jax.sharding import PartitionSpec as P

HD = 128
MESH = pl.DeviceIdType.MESH
SIDE = 8
N_DP = 64
TENSOR = 8
VIS = 64
TXT = 8
HEADS = 8
ROWS = HEADS * TXT
BLOCK = ROWS + 2 * TXT
KEYS = VIS + 2 * TXT
CHUNK = 4
SLOTS = N_DP
SCALE = HD ** (-0.5)

NT = (((1,), (1,)), ((), ()))
NN = (((1,), (0,)), ((), ()))
TN = (((0,), (0,)), ((), ()))


def dot(left, right, dims):
    return lax.dot_general(left, right, dims, preferred_element_type=jnp.float32)


def offset(group, turn):
    traced = not isinstance(group, int)
    a, b = (1 + lax.rem(group, 4), 3 - lax.div(group, 4)) if traced else (1 + group % 4, 3 - group // 4)
    last = lax.div(group, 15) if traced else group // 15
    if turn == 0:
        return a, b
    if turn == 1:
        return b, -a
    if turn == 2:
        return -a, -b + 4 * last
    return -b, a - 4 * last


def kernel(
    queries, text_kv, visual_kv, gain, images, rows_of, lengths,
    vis_out, back_recv, loss_out, owner_out,
    q_ref, text_ref, kv_ref, gain_ref, image_ref, length_ref, rows, meta_vec, meta,
    send_buf, recv_buf, key4, val4, acc, back_send, loss_send, loss_recv, loss_parts,
    load_sem, send_sem, recv_sem, back_send_sem, back_recv_sem, loss_send_sem, loss_recv_sem, part_send_sem, part_recv_sem,
):
    me = lax.axis_index("dp")
    core = lax.axis_index("tensor")
    z, y = lax.div(me, SIDE), lax.rem(me, SIDE)

    ahead_z = [lax.rem(z + step, SIDE) for step in range(SIDE)]
    ahead_y = [lax.rem(y + step, SIDE) for step in range(SIDE)]

    def target(group, turn):
        dz, dy = offset(group, turn)
        return ahead_z[dz % SIDE] * SIDE + ahead_y[dy % SIDE]

    def origin(group, turn):
        dz, dy = offset(group, turn)
        return lax.rem(z - dz + SIDE, SIDE), lax.rem(y - dy + SIDE, SIDE)

    pairs = [
        (images, image_ref), (lengths, length_ref), (rows_of, rows), (queries, q_ref), (text_kv, text_ref),
        (visual_kv, kv_ref), (gain, gain_ref),
    ]
    loads = [pltpu.make_async_copy(src, dst, load_sem.at[n]) for n, (src, dst) in enumerate(pairs)]
    for load in loads:
        load.start()

    barrier = pltpu.get_barrier_semaphore()

    def greet(step, carry):
        peer = lax.rem(me + step, N_DP)
        pl.semaphore_signal(barrier, inc=1, device_id=(peer, core), device_id_type=MESH)
        return carry

    lax.fori_loop(1, N_DP, greet, 0)
    for step in range(1, TENSOR):
        pl.semaphore_signal(barrier, inc=1, device_id=(me, (core + step) % TENSOR), device_id_type=MESH)

    loads[0].wait()
    loads[1].wait()
    half = me % 2
    lane128 = lax.broadcasted_iota(jnp.int32, (HD, HD), 1)
    row128 = lax.broadcasted_iota(jnp.int32, (HD, HD), 0)
    owner_row = image_ref[pl.ds(me // 2, 1)] // 4
    own_lane = lane128 // N_DP == half
    chosen = (owner_row == row128) & own_lane
    index8 = (lax.broadcasted_iota(jnp.int32, (8, HD), 1) - N_DP * half).astype(jnp.float32).astype(jnp.bfloat16)
    response_of = dot(index8, chosen.astype(jnp.float32).astype(jnp.bfloat16), NT)
    image_table = image_ref[...]
    held = image_table // 4 == me
    local_image = image_table % 4
    code = jnp.where(held, local_image + 4 * length_ref[...], 0).astype(jnp.float32)
    loads[2].wait()
    first_row, first_col = lax.div(4 * me, HD), lax.rem(4 * me, HD)
    seen = jnp.zeros_like(image_table)
    for image in range(4):
        seen = jnp.where(local_image == image, rows[first_row, first_col + image], seen)
    seen = jnp.where(held, seen, 0).astype(jnp.float32)
    code = jnp.concatenate([code, seen, jnp.zeros((HD - 64, HD), jnp.float32)], axis=0).astype(jnp.bfloat16)
    part = lax.broadcasted_iota(jnp.int32, (8, HD), 1) // N_DP == lax.broadcasted_iota(jnp.int32, (8, HD), 0)
    codes = dot(part.astype(jnp.float32).astype(jnp.bfloat16), code, NT)
    meta_vec[0:8] = jnp.clip(response_of.astype(jnp.int32), 0, N_DP - 1)
    meta_vec[8:16] = jnp.clip(codes.astype(jnp.int32), 0, HD - 1)
    meta_vec[16:24] = jnp.broadcast_to(owner_row, (8, HD))
    owner_out[...] = jnp.where(half == 0, owner_row, pltpu.roll(owner_row, N_DP, 1))
    to_scalars = pltpu.make_async_copy(meta_vec, meta, load_sem.at[7])
    to_scalars.start()
    loads[3].wait()
    loads[4].wait()
    to_scalars.wait()

    def stage(slot, peer, where):
        response = jnp.clip(meta[0, peer], 0, N_DP - 1)
        wide = q_ref[response].astype(jnp.float32)
        stacked = jnp.concatenate([wide[:, h * HD : (h + 1) * HD] for h in range(HEADS)], axis=0)
        where[slot, 0:ROWS] = stacked.astype(jnp.bfloat16)
        text = text_ref[response].astype(jnp.float32)
        pair = jnp.concatenate([text[:, 0:HD], text[:, HD : 2 * HD]], axis=0)
        where[slot, ROWS:BLOCK] = pair.astype(jnp.bfloat16)

    def send(slot, peer):
        pltpu.make_async_remote_copy(
            src_ref=send_buf.at[slot],
            dst_ref=recv_buf.at[slot],
            send_sem=send_sem.at[slot // CHUNK],
            recv_sem=recv_sem.at[slot // CHUNK],
            device_id=(peer, core),
            device_id_type=MESH,
        ).start()

    pl.semaphore_wait(barrier, N_DP - 1 + TENSOR - 1)

    for group in range(15):
        for turn in range(4):
            slot, peer = 4 * group + turn, target(group, turn)
            stage(slot, peer, send_buf)
            send(slot, peer)
    for turn in range(3):
        stage(60 + turn, target(15, turn), send_buf)
        send(60 + turn, target(15, turn))
    stage(63, me, recv_buf)

    for load in loads[5:]:
        load.wait()
    for image in range(4):
        key4[image] = kv_ref[image, :, 0:HD]
        val4[image] = kv_ref[image, :, HD : 2 * HD]
    acc[...] = jnp.zeros_like(acc)
    per_row = jnp.concatenate([jnp.broadcast_to(gain_ref[h : h + 1], (TXT, HD)) for h in range(HEADS)] * 2, axis=0)
    gain_t = per_row.T

    lane = lax.broadcasted_iota(jnp.int32, (1, HD), 1)
    first = lane < ROWS
    step_of = lane % TXT
    row = lax.broadcasted_iota(jnp.int32, (VIS + TXT, HD), 0)

    def key_rows(both):
        return jnp.where(first, both[0 : VIS + TXT], both[KEYS : KEYS + VIS + TXT])

    def value_rows(both):
        both = [jnp.concatenate([both[b : b + VIS], both[b + VIS + TXT : b + KEYS]], axis=0) for b in (0, KEYS)]
        return jnp.where(first, both[0], both[1])

    none = jnp.zeros((TXT, HD), jnp.float32)

    def diagonal(parts):
        values = jnp.concatenate(parts, axis=0)
        zero = jnp.zeros_like(values)
        return jnp.concatenate([jnp.where(first, values, zero), jnp.where(first, zero, values)], axis=0).astype(
            jnp.bfloat16
        )

    def work(group):
        pairs = []
        for half_of in range(2):
            slot = 4 * group + 2 * half_of
            images, lengths, seen = [], [], []
            for i in range(2):
                from_z, from_y = origin(group, 2 * half_of + i)
                code_row, code_lane = 8 + lax.rem(from_y, 2), from_z * 4 + lax.div(from_y, 2)
                code = meta[code_row, code_lane]
                images.append(jnp.clip(lax.rem(code, 4), 0, 3))
                lengths.append(lax.div(code, 4))
                seen.append(meta[code_row, 32 + code_lane])
            blocks = [recv_buf[slot + i] for i in range(2)]
            texts = [block[ROWS:BLOCK] for block in blocks]
            queries = jnp.concatenate([block[0:ROWS] for block in blocks], axis=0)
            keys = jnp.concatenate([key4[images[0]], texts[0], key4[images[1]], texts[1]], axis=0)
            values = jnp.concatenate([val4[images[0]], texts[0], val4[images[1]], texts[1]], axis=0)
            length = jnp.where(first, lengths[0], lengths[1])
            visible = jnp.where(first, seen[0], seen[1])
            pairs.append((images, queries, keys, values, length, visible))
        scores = [dot(keys, queries, NT) for _, queries, keys, _, _, _ in pairs]
        probs = []
        for (_, _, _, _, length, visible), score in zip(pairs, scores):
            text_end = VIS + jnp.minimum(step_of + 1, length)
            allowed = (row < visible) | ((row >= VIS) & (row < text_end))
            score = jnp.where(allowed, key_rows(score) * SCALE, jnp.float32(-1e30))
            raw = jnp.exp(score - jnp.max(score, axis=0, keepdims=True))
            probs.append(raw * (1.0 / jnp.sum(raw, axis=0, keepdims=True)))
        probs2 = [diagonal([prob[0:VIS], none, prob[VIS:]]) for prob in probs]
        attended = [dot(pair[3], prob2, TN) for pair, prob2 in zip(pairs, probs2)]
        cots, deltas, losses = [], [], []
        for pair, out in zip(pairs, attended):
            live = (step_of < pair[4]).astype(jnp.float32)
            weighted = gain_t * out * live
            loss_row = jnp.sum(weighted * out, axis=0, keepdims=True) * (1.0 / (2.0 * TXT * HD))
            cot = weighted.astype(jnp.bfloat16)
            cots.append(cot)
            deltas.append(jnp.sum(cot.astype(jnp.float32) * out, axis=0, keepdims=True))
            zero = jnp.zeros_like(loss_row)
            losses += [jnp.where(first, loss_row, zero), jnp.where(first, zero, loss_row)]
        prob_grads = [dot(pair[3], cot, NN) for pair, cot in zip(pairs, cots)]
        value_grads = [dot(prob2, cot, NT) for prob2, cot in zip(probs2, cots)]
        key_grads = []
        for pair, prob, grad, delta in zip(pairs, probs, prob_grads, deltas):
            score_grad2 = diagonal([prob * (value_rows(grad) - delta), none])
            key_grads.append(dot(score_grad2, pair[1], NN) * SCALE)
        images, backs, visuals = [], [], []
        for pair, key_grad, value_grad in zip(pairs, key_grads, value_grads):
            images += pair[0]
            for base in (0, KEYS):
                text_grad = [key_grad[base + VIS : base + VIS + TXT], value_grad[base + VIS + TXT : base + KEYS]]
                backs.append(jnp.concatenate(text_grad, axis=0).astype(jnp.bfloat16))
                visual = [key_grad[base : base + VIS], value_grad[base : base + VIS]]
                visuals.append(jnp.concatenate(visual, axis=0).astype(jnp.bfloat16).astype(jnp.float32))
        for image in range(4):
            total = acc[image]
            for held_image, visual in zip(images, visuals):
                total = total + jnp.where(held_image == image, visual, 0.0)
            acc[image] = total
        return backs, losses

    def back(slot, peer):
        pltpu.make_async_remote_copy(
            src_ref=back_send.at[slot],
            dst_ref=back_recv.at[me],
            send_sem=back_send_sem.at[0],
            recv_sem=back_recv_sem.at[0],
            device_id=(peer, core),
            device_id_type=MESH,
        ).start()
        pltpu.make_async_remote_copy(
            src_ref=loss_send.at[pl.ds(slot, 1)],
            dst_ref=loss_recv.at[pl.ds(me, 1)],
            send_sem=loss_send_sem.at[0],
            recv_sem=loss_recv_sem.at[0],
            device_id=(peer, core),
            device_id_type=MESH,
        ).start()

    def arrived(first_slot, count, chunk):
        pltpu.make_async_remote_copy(
            src_ref=send_buf.at[pl.ds(first_slot, count)],
            dst_ref=recv_buf.at[pl.ds(first_slot, count)],
            send_sem=send_sem.at[chunk],
            recv_sem=recv_sem.at[chunk],
            device_id=(me, core),
            device_id_type=MESH,
        ).wait_recv()

    def group_step(group, carry):
        arrived(4 * group, CHUNK, group)
        backs, losses = work(group)
        for turn in range(4):
            back_send[4 * group + turn] = backs[turn]
            loss_send[pl.ds(4 * group + turn, 1)] = losses[turn]
        for turn in range(4):
            from_z, from_y = origin(group, turn)
            back(4 * group + turn, from_z * SIDE + from_y)
        return carry

    lax.fori_loop(0, 15, group_step, 0)
    arrived(60, 3, 15)
    backs, losses = work(15)
    for turn in range(3):
        back_send[60 + turn] = backs[turn]
        loss_send[pl.ds(60 + turn, 1)] = losses[turn]
    for turn in range(3):
        from_z, from_y = origin(15, turn)
        back(60 + turn, from_z * SIDE + from_y)
    back_recv[me] = backs[3]
    loss_recv[pl.ds(me, 1)] = losses[3]

    for image in range(4):
        total = acc[image]
        vis_out[image] = jnp.concatenate([total[0:VIS], total[VIS : 2 * VIS]], axis=1).astype(jnp.bfloat16)

    remote = SLOTS - 1
    losses_in = pltpu.make_async_remote_copy(
        src_ref=loss_send.at[pl.ds(0, remote)],
        dst_ref=loss_recv.at[pl.ds(0, remote)],
        send_sem=loss_send_sem.at[0],
        recv_sem=loss_recv_sem.at[0],
        device_id=(me, core),
        device_id_type=MESH,
    )
    losses_in.wait_recv()
    per_slot = jnp.sum(loss_recv[...], axis=1, keepdims=True)
    slot_id = lax.broadcasted_iota(jnp.int32, (SLOTS, HD), 0)
    mine = jnp.sum(jnp.where(slot_id == owner_row, per_slot, 0.0), axis=0, keepdims=True)
    loss_parts[core] = mine
    for step in range(1, TENSOR):
        pltpu.make_async_remote_copy(
            src_ref=loss_parts.at[core],
            dst_ref=loss_parts.at[core],
            send_sem=part_send_sem.at[step],
            recv_sem=part_recv_sem.at[step],
            device_id=(me, (core + step) % TENSOR),
            device_id_type=MESH,
        ).start()

    backs_in = pltpu.make_async_remote_copy(
        src_ref=back_send.at[pl.ds(0, remote)],
        dst_ref=back_recv.at[pl.ds(0, remote)],
        send_sem=back_send_sem.at[0],
        recv_sem=back_recv_sem.at[0],
        device_id=(me, core),
        device_id_type=MESH,
    )
    backs_in.wait_recv()

    total = mine
    for step in range(1, TENSOR):
        peer = (core + TENSOR - step) % TENSOR
        pltpu.make_async_remote_copy(
            src_ref=loss_parts.at[peer],
            dst_ref=loss_parts.at[peer],
            send_sem=part_send_sem.at[step],
            recv_sem=part_recv_sem.at[step],
            device_id=(me, core),
            device_id_type=MESH,
        ).wait()
        total = total + loss_parts[peer]
    loss_out[...] = jnp.where(half == 0, total, pltpu.roll(total, N_DP, 1))

    losses_in.wait_send()
    backs_in.wait_send()
    for chunk in range(SLOTS // CHUNK):
        count = CHUNK if chunk < 15 else CHUNK - 1
        pltpu.make_async_remote_copy(
            src_ref=send_buf.at[pl.ds(chunk * CHUNK, count)],
            dst_ref=recv_buf.at[pl.ds(chunk * CHUNK, count)],
            send_sem=send_sem.at[chunk],
            recv_sem=recv_sem.at[chunk],
            device_id=(me, core),
            device_id_type=MESH,
        ).wait_send()


def finish(owner, vis, back, loss, vis_out, text_out, loss_out):
    def place(response, carry):
        block = back[owner[0, response]].astype(jnp.float32)
        text_out[response] = jnp.concatenate([block[0:TXT], block[TXT : 2 * TXT]], axis=1).astype(jnp.bfloat16)
        return carry

    lax.fori_loop(0, N_DP, place, 0, unroll=8)
    vis_out[...] = vis[...]
    loss_out[...] = loss[0, 0:N_DP]


def local(queries, text_kv, visual_kv, loss_gain, response_image, visual_rows, text_length):
    vmem = pl.BlockSpec(memory_space=pltpu.VMEM)
    vis, back, loss, owner = pl.pallas_call(
        kernel,
        out_shape=(
            jax.ShapeDtypeStruct(visual_kv.shape, jnp.bfloat16),
            jax.ShapeDtypeStruct((SLOTS, 2 * TXT, HD), jnp.bfloat16),
            jax.ShapeDtypeStruct((1, HD), jnp.float32),
            jax.ShapeDtypeStruct((1, HD), jnp.int32),
        ),
        in_specs=[pl.BlockSpec(memory_space=pltpu.HBM)] * 7,
        out_specs=(vmem, vmem, vmem, vmem),
        scratch_shapes=[
            pltpu.VMEM(queries.shape, jnp.bfloat16),
            pltpu.VMEM(text_kv.shape, jnp.bfloat16),
            pltpu.VMEM(visual_kv.shape, jnp.bfloat16),
            pltpu.VMEM((HEADS, HD), jnp.float32),
            pltpu.VMEM((32, HD), jnp.int32),
            pltpu.VMEM((32, HD), jnp.int32),
            pltpu.SMEM((2, HD), jnp.int32),
            pltpu.VMEM((24, HD), jnp.int32),
            pltpu.SMEM((24, HD), jnp.int32),
            pltpu.VMEM((SLOTS, BLOCK, HD), jnp.bfloat16),
            pltpu.VMEM((SLOTS, BLOCK, HD), jnp.bfloat16),
            pltpu.VMEM((4, VIS, HD), jnp.bfloat16),
            pltpu.VMEM((4, VIS, HD), jnp.bfloat16),
            pltpu.VMEM((4, 2 * VIS, HD), jnp.float32),
            pltpu.VMEM((SLOTS, 2 * TXT, HD), jnp.bfloat16),
            pltpu.VMEM((SLOTS, HD), jnp.float32),
            pltpu.VMEM((SLOTS, HD), jnp.float32),
            pltpu.VMEM((TENSOR, 1, HD), jnp.float32),
            pltpu.SemaphoreType.DMA((8,)),
            pltpu.SemaphoreType.DMA((SLOTS // CHUNK,)),
            pltpu.SemaphoreType.DMA((SLOTS // CHUNK,)),
            pltpu.SemaphoreType.DMA((1,)),
            pltpu.SemaphoreType.DMA((1,)),
            pltpu.SemaphoreType.DMA((1,)),
            pltpu.SemaphoreType.DMA((1,)),
            pltpu.SemaphoreType.DMA((TENSOR,)),
            pltpu.SemaphoreType.DMA((TENSOR,)),
        ],
        compiler_params=pltpu.CompilerParams(
            collective_id=0, has_side_effects=True, vmem_limit_bytes=60 * 1024 * 1024
        ),
        cost_estimate=pl.CostEstimate(flops=400_000_000, bytes_accessed=2_000_000, transcendentals=300_000),
    )(
        queries,
        text_kv,
        visual_kv,
        loss_gain.reshape(HEADS, HD),
        response_image.reshape(32, HD),
        visual_rows.reshape(2, HD),
        text_length.reshape(32, HD),
    )
    return pl.pallas_call(
        finish,
        out_shape=(
            jax.ShapeDtypeStruct(visual_kv.shape, jnp.bfloat16),
            jax.ShapeDtypeStruct(text_kv.shape, jnp.bfloat16),
            jax.ShapeDtypeStruct((N_DP,), jnp.float32),
        ),
        in_specs=[pl.BlockSpec(memory_space=pltpu.SMEM), vmem, vmem, vmem],
        out_specs=(vmem, vmem, vmem),
    )(owner, vis, back, loss)


def solution(mesh):
    in_specs = (
        P("dp", None, "tensor"),
        P("dp", None, "tensor"),
        P("dp", None, "tensor"),
        P("tensor"),
        P(),
        P(),
        P(),
    )
    out_specs = (P("dp", None, "tensor"), P("dp", None, "tensor"), P("dp"))
    return jax.shard_map(local, mesh=mesh, in_specs=in_specs, out_specs=out_specs, check_vma=False)
```

```python
import functools

import jax
import jax.numpy as jnp
from jax import lax
from jax.experimental import pallas as pl
from jax.experimental.pallas import tpu as pltpu
from jax.sharding import PartitionSpec as P

HD = 128
MESH = pl.DeviceIdType.MESH
SIDE = 8
N_DP = 64
TENSOR = 8
VIS = 64
TXT = 8
HEADS = 8
ROWS = HEADS * TXT
BLOCK = ROWS + 2 * TXT
KEYS = VIS + 2 * TXT
CHUNK = 4
SLOTS = N_DP
SCALE = HD ** (-0.5)

NT = (((1,), (1,)), ((), ()))
NN = (((1,), (0,)), ((), ()))
TN = (((0,), (0,)), ((), ()))


def dot(left, right, dims):
    return lax.dot_general(left, right, dims, preferred_element_type=jnp.float32)


def turned(a, b):
    return ((a, b), (-a, -b), (b, -a), (-b, a))


TABLE = (((4, 4), (4, 0), (0, 4), (0, 0)),) + tuple(turned(*ab) for ab in ((4, 3), (1, 0), (3, 3), (2, 0), (4, 2), (1, 1), (2, 3), (3, 0), (3, 2), (2, 1), (4, 1), (1, 2), (1, 3), (3, 1), (2, 2)))


def offset(group, turn):
    return TABLE[group][turn]


def kernel(
    queries, text_kv, visual_kv, gain, images, rows_of, lengths,
    vis_out, back_recv, loss_out, owner_out,
    q_ref, text_ref, kv_ref, gain_ref, image_ref, length_ref, rows, meta_vec, meta,
    send_buf, recv_buf, key4, val4, acc, back_send, loss_send, loss_recv, loss_parts,
    load_sem, send_sem, recv_sem, back_send_sem, back_recv_sem, loss_send_sem, loss_recv_sem, part_send_sem, part_recv_sem,
):
    me = lax.axis_index("dp")
    core = lax.axis_index("tensor")
    z, y = lax.div(me, SIDE), lax.rem(me, SIDE)

    ahead_z = [lax.rem(z + step, SIDE) for step in range(SIDE)]
    ahead_y = [lax.rem(y + step, SIDE) for step in range(SIDE)]

    def target(group, turn):
        dz, dy = offset(group, turn)
        return ahead_z[dz % SIDE] * SIDE + ahead_y[dy % SIDE]

    def origin(group, turn):
        dz, dy = offset(group, turn)
        return lax.rem(z - dz + SIDE, SIDE), lax.rem(y - dy + SIDE, SIDE)

    pairs = [
        (images, image_ref), (lengths, length_ref), (rows_of, rows), (queries, q_ref), (text_kv, text_ref),
        (visual_kv, kv_ref), (gain, gain_ref),
    ]
    loads = [pltpu.make_async_copy(src, dst, load_sem.at[n]) for n, (src, dst) in enumerate(pairs)]
    for load in loads:
        load.start()

    barrier = pltpu.get_barrier_semaphore()

    def greet(step, carry):
        peer = lax.rem(me + step, N_DP)
        pl.semaphore_signal(barrier, inc=1, device_id=(peer, core), device_id_type=MESH)
        return carry

    lax.fori_loop(1, N_DP, greet, 0)
    for step in range(1, TENSOR):
        pl.semaphore_signal(barrier, inc=1, device_id=(me, (core + step) % TENSOR), device_id_type=MESH)

    loads[0].wait()
    loads[1].wait()
    half = me % 2
    lane128 = lax.broadcasted_iota(jnp.int32, (HD, HD), 1)
    row128 = lax.broadcasted_iota(jnp.int32, (HD, HD), 0)
    owner_row = image_ref[pl.ds(me // 2, 1)] // 4
    own_lane = lane128 // N_DP == half
    chosen = (owner_row == row128) & own_lane
    index8 = (lax.broadcasted_iota(jnp.int32, (8, HD), 1) - N_DP * half).astype(jnp.float32).astype(jnp.bfloat16)
    response_of = dot(index8, chosen.astype(jnp.float32).astype(jnp.bfloat16), NT)
    image_table = image_ref[...]
    held = image_table // 4 == me
    local_image = image_table % 4
    code = jnp.where(held, local_image + 4 * length_ref[...], 0).astype(jnp.float32)
    loads[2].wait()
    first_row, first_col = lax.div(4 * me, HD), lax.rem(4 * me, HD)
    seen = jnp.zeros_like(image_table)
    for image in range(4):
        seen = jnp.where(local_image == image, rows[first_row, first_col + image], seen)
    seen = jnp.where(held, seen, 0).astype(jnp.float32)
    code = jnp.concatenate([code, seen, jnp.zeros((HD - 64, HD), jnp.float32)], axis=0).astype(jnp.bfloat16)
    part = lax.broadcasted_iota(jnp.int32, (8, HD), 1) // N_DP == lax.broadcasted_iota(jnp.int32, (8, HD), 0)
    codes = dot(part.astype(jnp.float32).astype(jnp.bfloat16), code, NT)
    meta_vec[0:8] = jnp.clip(response_of.astype(jnp.int32), 0, N_DP - 1)
    meta_vec[8:16] = jnp.clip(codes.astype(jnp.int32), 0, HD - 1)
    meta_vec[16:24] = jnp.broadcast_to(owner_row, (8, HD))
    owner_out[...] = jnp.where(half == 0, owner_row, pltpu.roll(owner_row, N_DP, 1))
    to_scalars = pltpu.make_async_copy(meta_vec, meta, load_sem.at[7])
    to_scalars.start()
    loads[3].wait()
    loads[4].wait()
    to_scalars.wait()

    def stage(slot, peer, where):
        response = jnp.clip(meta[0, peer], 0, N_DP - 1)
        wide = q_ref[response].astype(jnp.float32)
        stacked = jnp.concatenate([wide[:, h * HD : (h + 1) * HD] for h in range(HEADS)], axis=0)
        where[slot, 0:ROWS] = stacked.astype(jnp.bfloat16)
        text = text_ref[response].astype(jnp.float32)
        pair = jnp.concatenate([text[:, 0:HD], text[:, HD : 2 * HD]], axis=0)
        where[slot, ROWS:BLOCK] = pair.astype(jnp.bfloat16)

    def send(slot, peer):
        pltpu.make_async_remote_copy(
            src_ref=send_buf.at[slot],
            dst_ref=recv_buf.at[slot],
            send_sem=send_sem.at[slot // CHUNK],
            recv_sem=recv_sem.at[slot // CHUNK],
            device_id=(peer, core),
            device_id_type=MESH,
        ).start()

    pl.semaphore_wait(barrier, N_DP - 1 + TENSOR - 1)

    for slot in range(SLOTS):
        if slot == 3:
            stage(slot, me, recv_buf)
        else:
            peer = target(slot // CHUNK, slot % CHUNK)
            stage(slot, peer, send_buf)
            send(slot, peer)

    for load in loads[5:]:
        load.wait()
    for image in range(4):
        key4[image] = kv_ref[image, :, 0:HD]
        val4[image] = kv_ref[image, :, HD : 2 * HD]
    acc[...] = jnp.zeros_like(acc)
    per_row = jnp.concatenate([jnp.broadcast_to(gain_ref[h : h + 1], (TXT, HD)) for h in range(HEADS)] * 2, axis=0)
    gain_t = per_row.T

    lane = lax.broadcasted_iota(jnp.int32, (1, HD), 1)
    first = lane < ROWS
    step_of = lane % TXT
    row = lax.broadcasted_iota(jnp.int32, (VIS + TXT, HD), 0)

    def key_rows(both):
        return jnp.where(first, both[0 : VIS + TXT], both[KEYS : KEYS + VIS + TXT])

    def value_rows(both):
        both = [jnp.concatenate([both[b : b + VIS], both[b + VIS + TXT : b + KEYS]], axis=0) for b in (0, KEYS)]
        return jnp.where(first, both[0], both[1])

    none = jnp.zeros((TXT, HD), jnp.float32)

    def diagonal(parts):
        values = jnp.concatenate(parts, axis=0)
        zero = jnp.zeros_like(values)
        return jnp.concatenate([jnp.where(first, values, zero), jnp.where(first, zero, values)], axis=0).astype(
            jnp.bfloat16
        )

    def work(group):
        pairs = []
        for half_of in range(2):
            slot = 4 * group + 2 * half_of
            images, lengths, seen = [], [], []
            for i in range(2):
                from_z, from_y = origin(group, 2 * half_of + i)
                code_row, code_lane = 8 + lax.rem(from_y, 2), from_z * 4 + lax.div(from_y, 2)
                code = meta[code_row, code_lane]
                images.append(jnp.clip(lax.rem(code, 4), 0, 3))
                lengths.append(lax.div(code, 4))
                seen.append(meta[code_row, 32 + code_lane])
            blocks = [recv_buf[slot + i] for i in range(2)]
            texts = [block[ROWS:BLOCK] for block in blocks]
            queries = jnp.concatenate([block[0:ROWS] for block in blocks], axis=0)
            keys = jnp.concatenate([key4[images[0]], texts[0], key4[images[1]], texts[1]], axis=0)
            values = jnp.concatenate([val4[images[0]], texts[0], val4[images[1]], texts[1]], axis=0)
            length = jnp.where(first, lengths[0], lengths[1])
            visible = jnp.where(first, seen[0], seen[1])
            pairs.append((images, queries, keys, values, length, visible))
        scores = [dot(keys, queries, NT) for _, queries, keys, _, _, _ in pairs]
        probs = []
        for (_, _, _, _, length, visible), score in zip(pairs, scores):
            text_end = VIS + jnp.minimum(step_of + 1, length)
            allowed = (row < visible) | ((row >= VIS) & (row < text_end))
            score = jnp.where(allowed, key_rows(score) * SCALE, jnp.float32(-1e30))
            raw = jnp.exp(score - jnp.max(score, axis=0, keepdims=True))
            probs.append(raw * (1.0 / jnp.sum(raw, axis=0, keepdims=True)))
        probs2 = [diagonal([prob[0:VIS], none, prob[VIS:]]) for prob in probs]
        attended = [dot(pair[3], prob2, TN) for pair, prob2 in zip(pairs, probs2)]
        cots, deltas, losses = [], [], []
        for pair, out in zip(pairs, attended):
            live = (step_of < pair[4]).astype(jnp.float32)
            weighted = gain_t * out * live
            loss_row = jnp.sum(weighted * out, axis=0, keepdims=True) * (1.0 / (2.0 * TXT * HD))
            cot = weighted.astype(jnp.bfloat16)
            cots.append(cot)
            deltas.append(jnp.sum(cot.astype(jnp.float32) * out, axis=0, keepdims=True))
            zero = jnp.zeros_like(loss_row)
            losses += [jnp.where(first, loss_row, zero), jnp.where(first, zero, loss_row)]
        prob_grads = [dot(pair[3], cot, NN) for pair, cot in zip(pairs, cots)]
        value_grads = [dot(prob2, cot, NT) for prob2, cot in zip(probs2, cots)]
        key_grads = []
        for pair, prob, grad, delta in zip(pairs, probs, prob_grads, deltas):
            score_grad2 = diagonal([prob * (value_rows(grad) - delta), none])
            key_grads.append(dot(score_grad2, pair[1], NN) * SCALE)
        images, backs, visuals = [], [], []
        for pair, key_grad, value_grad in zip(pairs, key_grads, value_grads):
            images += pair[0]
            for base in (0, KEYS):
                text_grad = [key_grad[base + VIS : base + VIS + TXT], value_grad[base + VIS + TXT : base + KEYS]]
                backs.append(jnp.concatenate(text_grad, axis=0).astype(jnp.bfloat16))
                visual = [key_grad[base : base + VIS], value_grad[base : base + VIS]]
                visuals.append(jnp.concatenate(visual, axis=0).astype(jnp.bfloat16).astype(jnp.float32))
        for image in range(4):
            total = acc[image]
            for held_image, visual in zip(images, visuals):
                total = total + jnp.where(held_image == image, visual, 0.0)
            acc[image] = total
        return backs, losses

    def back(slot, peer):
        pltpu.make_async_remote_copy(
            src_ref=back_send.at[slot],
            dst_ref=back_recv.at[me],
            send_sem=back_send_sem.at[0],
            recv_sem=back_recv_sem.at[0],
            device_id=(peer, core),
            device_id_type=MESH,
        ).start()
        pltpu.make_async_remote_copy(
            src_ref=loss_send.at[pl.ds(slot, 1)],
            dst_ref=loss_recv.at[pl.ds(me, 1)],
            send_sem=loss_send_sem.at[0],
            recv_sem=loss_recv_sem.at[0],
            device_id=(peer, core),
            device_id_type=MESH,
        ).start()

    def arrived(first_slot, count, chunk):
        pltpu.make_async_remote_copy(
            src_ref=send_buf.at[pl.ds(first_slot, count)],
            dst_ref=recv_buf.at[pl.ds(first_slot, count)],
            send_sem=send_sem.at[chunk],
            recv_sem=recv_sem.at[chunk],
            device_id=(me, core),
            device_id_type=MESH,
        ).wait_recv()

    def group_step(group, carry):
        arrived(4 * group, CHUNK, group)
        backs, losses = work(group)
        for turn in range(4):
            back_send[4 * group + turn] = backs[turn]
            loss_send[pl.ds(4 * group + turn, 1)] = losses[turn]
        for turn in range(4):
            from_z, from_y = origin(group, turn)
            back(4 * group + turn, from_z * SIDE + from_y)
        return carry

    for group in range(16):
        if group != 0:
            group_step(group, 0)
            continue
        arrived(4 * group, 3, group)
        backs, losses = work(group)
        for turn in range(3):
            back_send[4 * group + turn] = backs[turn]
            loss_send[pl.ds(4 * group + turn, 1)] = losses[turn]
        for turn in range(3):
            from_z, from_y = origin(group, turn)
            back(4 * group + turn, from_z * SIDE + from_y)
        back_recv[me] = backs[3]
        loss_recv[pl.ds(me, 1)] = losses[3]

    for image in range(4):
        total = acc[image]
        vis_out[image] = jnp.concatenate([total[0:VIS], total[VIS : 2 * VIS]], axis=1).astype(jnp.bfloat16)

    remote = SLOTS - 1
    losses_in = pltpu.make_async_remote_copy(
        src_ref=loss_send.at[pl.ds(0, remote)],
        dst_ref=loss_recv.at[pl.ds(0, remote)],
        send_sem=loss_send_sem.at[0],
        recv_sem=loss_recv_sem.at[0],
        device_id=(me, core),
        device_id_type=MESH,
    )
    losses_in.wait_recv()
    per_slot = jnp.sum(loss_recv[...], axis=1, keepdims=True)
    slot_id = lax.broadcasted_iota(jnp.int32, (SLOTS, HD), 0)
    mine = jnp.sum(jnp.where(slot_id == owner_row, per_slot, 0.0), axis=0, keepdims=True)
    loss_parts[core] = mine
    for step in range(1, TENSOR):
        pltpu.make_async_remote_copy(
            src_ref=loss_parts.at[core],
            dst_ref=loss_parts.at[core],
            send_sem=part_send_sem.at[step],
            recv_sem=part_recv_sem.at[step],
            device_id=(me, (core + step) % TENSOR),
            device_id_type=MESH,
        ).start()

    backs_in = pltpu.make_async_remote_copy(
        src_ref=back_send.at[pl.ds(0, remote)],
        dst_ref=back_recv.at[pl.ds(0, remote)],
        send_sem=back_send_sem.at[0],
        recv_sem=back_recv_sem.at[0],
        device_id=(me, core),
        device_id_type=MESH,
    )
    backs_in.wait_recv()

    total = mine
    for step in range(1, TENSOR):
        peer = (core + TENSOR - step) % TENSOR
        pltpu.make_async_remote_copy(
            src_ref=loss_parts.at[peer],
            dst_ref=loss_parts.at[peer],
            send_sem=part_send_sem.at[step],
            recv_sem=part_recv_sem.at[step],
            device_id=(me, core),
            device_id_type=MESH,
        ).wait()
        total = total + loss_parts[peer]
    loss_out[...] = jnp.where(half == 0, total, pltpu.roll(total, N_DP, 1))

    losses_in.wait_send()
    backs_in.wait_send()
    for chunk in range(SLOTS // CHUNK):
        count = CHUNK if chunk != 0 else 3
        pltpu.make_async_remote_copy(
            src_ref=send_buf.at[pl.ds(chunk * CHUNK, count)],
            dst_ref=recv_buf.at[pl.ds(chunk * CHUNK, count)],
            send_sem=send_sem.at[chunk],
            recv_sem=recv_sem.at[chunk],
            device_id=(me, core),
            device_id_type=MESH,
        ).wait_send()


def finish(owner, vis, back, loss, vis_out, text_out, loss_out):
    def place(response, carry):
        block = back[owner[0, response]].astype(jnp.float32)
        text_out[response] = jnp.concatenate([block[0:TXT], block[TXT : 2 * TXT]], axis=1).astype(jnp.bfloat16)
        return carry

    lax.fori_loop(0, N_DP, place, 0, unroll=8)
    vis_out[...] = vis[...]
    loss_out[...] = loss[0, 0:N_DP]


def local(queries, text_kv, visual_kv, loss_gain, response_image, visual_rows, text_length):
    vmem = pl.BlockSpec(memory_space=pltpu.VMEM)
    vis, back, loss, owner = pl.pallas_call(
        kernel,
        out_shape=(
            jax.ShapeDtypeStruct(visual_kv.shape, jnp.bfloat16),
            jax.ShapeDtypeStruct((SLOTS, 2 * TXT, HD), jnp.bfloat16),
            jax.ShapeDtypeStruct((1, HD), jnp.float32),
            jax.ShapeDtypeStruct((1, HD), jnp.int32),
        ),
        in_specs=[pl.BlockSpec(memory_space=pltpu.HBM)] * 7,
        out_specs=(vmem, vmem, vmem, vmem),
        scratch_shapes=[
            pltpu.VMEM(queries.shape, jnp.bfloat16),
            pltpu.VMEM(text_kv.shape, jnp.bfloat16),
            pltpu.VMEM(visual_kv.shape, jnp.bfloat16),
            pltpu.VMEM((HEADS, HD), jnp.float32),
            pltpu.VMEM((32, HD), jnp.int32),
            pltpu.VMEM((32, HD), jnp.int32),
            pltpu.SMEM((2, HD), jnp.int32),
            pltpu.VMEM((24, HD), jnp.int32),
            pltpu.SMEM((24, HD), jnp.int32),
            pltpu.VMEM((SLOTS, BLOCK, HD), jnp.bfloat16),
            pltpu.VMEM((SLOTS, BLOCK, HD), jnp.bfloat16),
            pltpu.VMEM((4, VIS, HD), jnp.bfloat16),
            pltpu.VMEM((4, VIS, HD), jnp.bfloat16),
            pltpu.VMEM((4, 2 * VIS, HD), jnp.float32),
            pltpu.VMEM((SLOTS, 2 * TXT, HD), jnp.bfloat16),
            pltpu.VMEM((SLOTS, HD), jnp.float32),
            pltpu.VMEM((SLOTS, HD), jnp.float32),
            pltpu.VMEM((TENSOR, 1, HD), jnp.float32),
            pltpu.SemaphoreType.DMA((8,)),
            pltpu.SemaphoreType.DMA((SLOTS // CHUNK,)),
            pltpu.SemaphoreType.DMA((SLOTS // CHUNK,)),
            pltpu.SemaphoreType.DMA((1,)),
            pltpu.SemaphoreType.DMA((1,)),
            pltpu.SemaphoreType.DMA((1,)),
            pltpu.SemaphoreType.DMA((1,)),
            pltpu.SemaphoreType.DMA((TENSOR,)),
            pltpu.SemaphoreType.DMA((TENSOR,)),
        ],
        compiler_params=pltpu.CompilerParams(
            collective_id=0, has_side_effects=True, vmem_limit_bytes=60 * 1024 * 1024
        ),
        cost_estimate=pl.CostEstimate(flops=400_000_000, bytes_accessed=2_000_000, transcendentals=300_000),
    )(
        queries,
        text_kv,
        visual_kv,
        loss_gain.reshape(HEADS, HD),
        response_image.reshape(32, HD),
        visual_rows.reshape(2, HD),
        text_length.reshape(32, HD),
    )
    return pl.pallas_call(
        finish,
        out_shape=(
            jax.ShapeDtypeStruct(visual_kv.shape, jnp.bfloat16),
            jax.ShapeDtypeStruct(text_kv.shape, jnp.bfloat16),
            jax.ShapeDtypeStruct((N_DP,), jnp.float32),
        ),
        in_specs=[pl.BlockSpec(memory_space=pltpu.SMEM), vmem, vmem, vmem],
        out_specs=(vmem, vmem, vmem),
    )(owner, vis, back, loss)


def solution(mesh):
    in_specs = (
        P("dp", None, "tensor"),
        P("dp", None, "tensor"),
        P("dp", None, "tensor"),
        P("tensor"),
        P(),
        P(),
        P(),
    )
    out_specs = (P("dp", None, "tensor"), P("dp", None, "tensor"), P("dp"))
    return jax.shard_map(local, mesh=mesh, in_specs=in_specs, out_specs=out_specs, check_vma=False)
```

```python
import functools

import jax
import jax.numpy as jnp
from jax import lax
from jax.experimental import pallas as pl
from jax.experimental.pallas import tpu as pltpu
from jax.sharding import PartitionSpec as P

HD = 128
MESH = pl.DeviceIdType.MESH
SIDE = 8
N_DP = 64
TENSOR = 8
VIS = 64
TXT = 8
HEADS = 8
ROWS = HEADS * TXT
BLOCK = ROWS + 2 * TXT
KEYS = VIS + 2 * TXT
CHUNK = 4
SLOTS = N_DP
SELF = 3
SCALE = HD ** (-0.5)

NT = (((1,), (1,)), ((), ()))
NN = (((1,), (0,)), ((), ()))
TN = (((0,), (0,)), ((), ()))


def dot(left, right, dims):
    return lax.dot_general(left, right, dims, preferred_element_type=jnp.float32)


def turned(a, b):
    return ((a, b), (-a, -b), (b, -a), (-b, a))


TABLE = (((4, 4), (4, 0), (0, 4), (0, 0)),) + tuple(turned(*ab) for ab in ((4, 3), (1, 0), (3, 3), (2, 0), (4, 2), (1, 1), (2, 3), (3, 0), (3, 2), (2, 1), (4, 1), (1, 2), (1, 3), (3, 1), (2, 2)))


def offset(group, turn):
    return TABLE[group][turn]


def kernel(
    queries, text_kv, visual_kv, gain, images, rows_of, lengths,
    vis_out, back_recv, loss_out, owner_out,
    q_ref, text_ref, kv_ref, gain_ref, image_ref, length_ref, rows, meta_vec, meta,
    send_buf, recv_buf, key4, val4, acc, back_send, loss_send, loss_recv, loss_parts,
    load_sem, send_sem, recv_sem, back_send_sem, back_recv_sem, loss_send_sem, loss_recv_sem, part_send_sem, part_recv_sem,
):
    me = lax.axis_index("dp")
    core = lax.axis_index("tensor")
    z, y = lax.div(me, SIDE), lax.rem(me, SIDE)

    ahead_z = [lax.rem(z + step, SIDE) for step in range(SIDE)]
    ahead_y = [lax.rem(y + step, SIDE) for step in range(SIDE)]

    def target(group, turn):
        dz, dy = offset(group, turn)
        return ahead_z[dz % SIDE] * SIDE + ahead_y[dy % SIDE]

    def origin(group, turn):
        dz, dy = offset(group, turn)
        return lax.rem(z - dz + SIDE, SIDE), lax.rem(y - dy + SIDE, SIDE)

    pairs = [
        (images, image_ref), (lengths, length_ref), (rows_of, rows), (queries, q_ref), (text_kv, text_ref),
        (visual_kv, kv_ref), (gain, gain_ref),
    ]
    loads = [pltpu.make_async_copy(src, dst, load_sem.at[n]) for n, (src, dst) in enumerate(pairs)]
    for load in loads:
        load.start()

    barrier = pltpu.get_barrier_semaphore()

    def greet(step, carry):
        peer = lax.rem(me + step, N_DP)
        pl.semaphore_signal(barrier, inc=1, device_id=(peer, core), device_id_type=MESH)
        return carry

    lax.fori_loop(1, N_DP, greet, 0)
    for step in range(1, TENSOR):
        pl.semaphore_signal(barrier, inc=1, device_id=(me, (core + step) % TENSOR), device_id_type=MESH)

    loads[0].wait()
    loads[1].wait()
    half = me % 2
    lane128 = lax.broadcasted_iota(jnp.int32, (HD, HD), 1)
    row128 = lax.broadcasted_iota(jnp.int32, (HD, HD), 0)
    owner_row = image_ref[pl.ds(me // 2, 1)] // 4
    own_lane = lane128 // N_DP == half
    chosen = (owner_row == row128) & own_lane
    index8 = (lax.broadcasted_iota(jnp.int32, (8, HD), 1) - N_DP * half).astype(jnp.float32).astype(jnp.bfloat16)
    response_of = dot(index8, chosen.astype(jnp.float32).astype(jnp.bfloat16), NT)
    image_table = image_ref[...]
    held = image_table // 4 == me
    local_image = image_table % 4
    code = jnp.where(held, local_image + 4 * length_ref[...], 0).astype(jnp.float32)
    loads[2].wait()
    first_row, first_col = lax.div(4 * me, HD), lax.rem(4 * me, HD)
    seen = jnp.zeros_like(image_table)
    for image in range(4):
        seen = jnp.where(local_image == image, rows[first_row, first_col + image], seen)
    seen = jnp.where(held, seen, 0).astype(jnp.float32)
    code = jnp.concatenate([code, seen, jnp.zeros((HD - 64, HD), jnp.float32)], axis=0).astype(jnp.bfloat16)
    part = lax.broadcasted_iota(jnp.int32, (8, HD), 1) // N_DP == lax.broadcasted_iota(jnp.int32, (8, HD), 0)
    codes = dot(part.astype(jnp.float32).astype(jnp.bfloat16), code, NT)
    meta_vec[0:8] = jnp.clip(response_of.astype(jnp.int32), 0, N_DP - 1)
    meta_vec[8:16] = jnp.clip(codes.astype(jnp.int32), 0, HD - 1)
    meta_vec[16:24] = jnp.broadcast_to(owner_row, (8, HD))
    owner_out[...] = jnp.where(half == 0, owner_row, pltpu.roll(owner_row, N_DP, 1))
    to_scalars = pltpu.make_async_copy(meta_vec, meta, load_sem.at[7])
    to_scalars.start()
    loads[3].wait()
    loads[4].wait()
    to_scalars.wait()

    def stage(slot, peer, where):
        response = jnp.clip(meta[0, peer], 0, N_DP - 1)
        wide = q_ref[response].astype(jnp.float32)
        stacked = jnp.concatenate([wide[:, h * HD : (h + 1) * HD] for h in range(HEADS)], axis=0)
        where[slot, 0:ROWS] = stacked.astype(jnp.bfloat16)
        text = text_ref[response].astype(jnp.float32)
        pair = jnp.concatenate([text[:, 0:HD], text[:, HD : 2 * HD]], axis=0)
        where[slot, ROWS:BLOCK] = pair.astype(jnp.bfloat16)

    def send(slot, peer):
        pltpu.make_async_remote_copy(
            src_ref=send_buf.at[slot],
            dst_ref=recv_buf.at[slot],
            send_sem=send_sem.at[slot // CHUNK],
            recv_sem=recv_sem.at[slot // CHUNK],
            device_id=(peer, core),
            device_id_type=MESH,
        ).start()

    pl.semaphore_wait(barrier, N_DP - 1 + TENSOR - 1)

    for slot in range(SLOTS):
        if slot == 3:
            stage(slot, me, recv_buf)
        else:
            peer = target(slot // CHUNK, slot % CHUNK)
            stage(slot, peer, send_buf)
            send(slot, peer)

    for load in loads[5:]:
        load.wait()
    for image in range(4):
        key4[image] = kv_ref[image, :, 0:HD]
        val4[image] = kv_ref[image, :, HD : 2 * HD]
    acc[...] = jnp.zeros_like(acc)
    per_row = jnp.concatenate([jnp.broadcast_to(gain_ref[h : h + 1], (TXT, HD)) for h in range(HEADS)] * 2, axis=0)
    gain_t = per_row.T

    lane = lax.broadcasted_iota(jnp.int32, (1, HD), 1)
    first = lane < ROWS
    step_of = lane % TXT
    row = lax.broadcasted_iota(jnp.int32, (VIS + TXT, HD), 0)

    def key_rows(both):
        return jnp.where(first, both[0 : VIS + TXT], both[KEYS : KEYS + VIS + TXT])

    def value_rows(both):
        both = [jnp.concatenate([both[b : b + VIS], both[b + VIS + TXT : b + KEYS]], axis=0) for b in (0, KEYS)]
        return jnp.where(first, both[0], both[1])

    none = jnp.zeros((TXT, HD), jnp.float32)

    def diagonal(parts):
        values = jnp.concatenate(parts, axis=0)
        zero = jnp.zeros_like(values)
        return jnp.concatenate([jnp.where(first, values, zero), jnp.where(first, zero, values)], axis=0).astype(
            jnp.bfloat16
        )

    def work(group):
        pairs = []
        for half_of in range(2):
            slot = 4 * group + 2 * half_of
            images, lengths, seen = [], [], []
            for i in range(2):
                from_z, from_y = origin(group, 2 * half_of + i)
                code_row, code_lane = 8 + lax.rem(from_y, 2), from_z * 4 + lax.div(from_y, 2)
                code = meta[code_row, code_lane]
                images.append(jnp.clip(lax.rem(code, 4), 0, 3))
                lengths.append(lax.div(code, 4))
                seen.append(meta[code_row, 32 + code_lane])
            blocks = [recv_buf[slot + i] for i in range(2)]
            texts = [block[ROWS:BLOCK] for block in blocks]
            queries = jnp.concatenate([block[0:ROWS] for block in blocks], axis=0)
            keys = jnp.concatenate([key4[images[0]], texts[0], key4[images[1]], texts[1]], axis=0)
            values = jnp.concatenate([val4[images[0]], texts[0], val4[images[1]], texts[1]], axis=0)
            length = jnp.where(first, lengths[0], lengths[1])
            visible = jnp.where(first, seen[0], seen[1])
            pairs.append((images, queries, keys, values, length, visible))
        scores = [dot(keys, queries, NT) for _, queries, keys, _, _, _ in pairs]
        probs = []
        for (_, _, _, _, length, visible), score in zip(pairs, scores):
            text_end = VIS + jnp.minimum(step_of + 1, length)
            allowed = (row < visible) | ((row >= VIS) & (row < text_end))
            score = jnp.where(allowed, key_rows(score) * SCALE, jnp.float32(-1e30))
            raw = jnp.exp(score - jnp.max(score, axis=0, keepdims=True))
            probs.append(raw * (1.0 / jnp.sum(raw, axis=0, keepdims=True)))
        probs2 = [diagonal([prob[0:VIS], none, prob[VIS:]]) for prob in probs]
        attended = [dot(pair[3], prob2, TN) for pair, prob2 in zip(pairs, probs2)]
        cots, deltas, losses = [], [], []
        for pair, out in zip(pairs, attended):
            live = (step_of < pair[4]).astype(jnp.float32)
            weighted = gain_t * out * live
            loss_row = jnp.sum(weighted * out, axis=0, keepdims=True) * (1.0 / (2.0 * TXT * HD))
            cot = weighted.astype(jnp.bfloat16)
            cots.append(cot)
            deltas.append(jnp.sum(cot.astype(jnp.float32) * out, axis=0, keepdims=True))
            zero = jnp.zeros_like(loss_row)
            losses += [jnp.where(first, loss_row, zero), jnp.where(first, zero, loss_row)]
        prob_grads = [dot(pair[3], cot, NN) for pair, cot in zip(pairs, cots)]
        value_grads = [dot(prob2, cot, NT) for prob2, cot in zip(probs2, cots)]
        key_grads = []
        for pair, prob, grad, delta in zip(pairs, probs, prob_grads, deltas):
            score_grad2 = diagonal([prob * (value_rows(grad) - delta), none])
            key_grads.append(dot(score_grad2, pair[1], NN) * SCALE)
        images, backs, visuals = [], [], []
        for pair, key_grad, value_grad in zip(pairs, key_grads, value_grads):
            images += pair[0]
            for base in (0, KEYS):
                text_grad = [key_grad[base + VIS : base + VIS + TXT], value_grad[base + VIS + TXT : base + KEYS]]
                backs.append(jnp.concatenate(text_grad, axis=0).astype(jnp.bfloat16))
                visual = [key_grad[base : base + VIS], value_grad[base : base + VIS]]
                visuals.append(jnp.concatenate(visual, axis=0).astype(jnp.bfloat16).astype(jnp.float32))
        for image in range(4):
            total = acc[image]
            for held_image, visual in zip(images, visuals):
                total = total + jnp.where(held_image == image, visual, 0.0)
            acc[image] = total
        return backs, losses

    def back(slot, peer):
        pltpu.make_async_remote_copy(
            src_ref=back_send.at[slot],
            dst_ref=back_recv.at[me],
            send_sem=back_send_sem.at[0],
            recv_sem=back_recv_sem.at[0],
            device_id=(peer, core),
            device_id_type=MESH,
        ).start()

    def back_loss(slot, peer):
        pltpu.make_async_remote_copy(
            src_ref=loss_send.at[pl.ds(slot, 1)],
            dst_ref=loss_recv.at[pl.ds(me, 1)],
            send_sem=loss_send_sem.at[0],
            recv_sem=loss_recv_sem.at[0],
            device_id=(peer, core),
            device_id_type=MESH,
        ).start()

    def arrived(first_slot, count, chunk):
        pltpu.make_async_remote_copy(
            src_ref=send_buf.at[pl.ds(first_slot, count)],
            dst_ref=recv_buf.at[pl.ds(first_slot, count)],
            send_sem=send_sem.at[chunk],
            recv_sem=recv_sem.at[chunk],
            device_id=(me, core),
            device_id_type=MESH,
        ).wait_recv()

    def give_back(group):
        for turn in range(CHUNK if group else SELF):
            from_z, from_y = origin(group, turn)
            back(4 * group + turn, from_z * SIDE + from_y)

    for group in range(16):
        count = CHUNK if group else SELF
        arrived(4 * group, count, group)
        backs, losses = work(group)
        for turn in range(count):
            back_send[4 * group + turn] = backs[turn]
            loss_send[pl.ds(4 * group + turn, 1)] = losses[turn]
        if group == 0:
            back_recv[me] = backs[SELF]
            loss_recv[pl.ds(me, 1)] = losses[SELF]
        for turn in range(count):
            from_z, from_y = origin(group, turn)
            back_loss(4 * group + turn, from_z * SIDE + from_y)
    for group in sorted(range(16), key=lambda group: -sum(abs(step) for step in TABLE[group][0])):
        give_back(group)

    for image in range(4):
        total = acc[image]
        vis_out[image] = jnp.concatenate([total[0:VIS], total[VIS : 2 * VIS]], axis=1).astype(jnp.bfloat16)

    remote = SLOTS - 1
    losses_in = pltpu.make_async_remote_copy(
        src_ref=loss_send.at[pl.ds(0, remote)],
        dst_ref=loss_recv.at[pl.ds(0, remote)],
        send_sem=loss_send_sem.at[0],
        recv_sem=loss_recv_sem.at[0],
        device_id=(me, core),
        device_id_type=MESH,
    )
    losses_in.wait_recv()
    per_slot = jnp.sum(loss_recv[...], axis=1, keepdims=True)
    slot_id = lax.broadcasted_iota(jnp.int32, (SLOTS, HD), 0)
    mine = jnp.sum(jnp.where(slot_id == owner_row, per_slot, 0.0), axis=0, keepdims=True)
    loss_parts[core] = mine
    for step in range(1, TENSOR):
        pltpu.make_async_remote_copy(
            src_ref=loss_parts.at[core],
            dst_ref=loss_parts.at[core],
            send_sem=part_send_sem.at[step],
            recv_sem=part_recv_sem.at[step],
            device_id=(me, (core + step) % TENSOR),
            device_id_type=MESH,
        ).start()

    backs_in = pltpu.make_async_remote_copy(
        src_ref=back_send.at[pl.ds(0, remote)],
        dst_ref=back_recv.at[pl.ds(0, remote)],
        send_sem=back_send_sem.at[0],
        recv_sem=back_recv_sem.at[0],
        device_id=(me, core),
        device_id_type=MESH,
    )
    backs_in.wait_recv()

    total = mine
    for step in range(1, TENSOR):
        peer = (core + TENSOR - step) % TENSOR
        pltpu.make_async_remote_copy(
            src_ref=loss_parts.at[peer],
            dst_ref=loss_parts.at[peer],
            send_sem=part_send_sem.at[step],
            recv_sem=part_recv_sem.at[step],
            device_id=(me, core),
            device_id_type=MESH,
        ).wait()
        total = total + loss_parts[peer]
    loss_out[...] = jnp.where(half == 0, total, pltpu.roll(total, N_DP, 1))

    losses_in.wait_send()
    backs_in.wait_send()
    for chunk in range(SLOTS // CHUNK):
        count = CHUNK if chunk != 0 else 3
        pltpu.make_async_remote_copy(
            src_ref=send_buf.at[pl.ds(chunk * CHUNK, count)],
            dst_ref=recv_buf.at[pl.ds(chunk * CHUNK, count)],
            send_sem=send_sem.at[chunk],
            recv_sem=recv_sem.at[chunk],
            device_id=(me, core),
            device_id_type=MESH,
        ).wait_send()


def finish(owner, vis, back, loss, vis_out, text_out, loss_out):
    def place(response, carry):
        block = back[owner[0, response]].astype(jnp.float32)
        text_out[response] = jnp.concatenate([block[0:TXT], block[TXT : 2 * TXT]], axis=1).astype(jnp.bfloat16)
        return carry

    lax.fori_loop(0, N_DP, place, 0, unroll=8)
    vis_out[...] = vis[...]
    loss_out[...] = loss[0, 0:N_DP]


def local(queries, text_kv, visual_kv, loss_gain, response_image, visual_rows, text_length):
    vmem = pl.BlockSpec(memory_space=pltpu.VMEM)
    vis, back, loss, owner = pl.pallas_call(
        kernel,
        out_shape=(
            jax.ShapeDtypeStruct(visual_kv.shape, jnp.bfloat16),
            jax.ShapeDtypeStruct((SLOTS, 2 * TXT, HD), jnp.bfloat16),
            jax.ShapeDtypeStruct((1, HD), jnp.float32),
            jax.ShapeDtypeStruct((1, HD), jnp.int32),
        ),
        in_specs=[pl.BlockSpec(memory_space=pltpu.HBM)] * 7,
        out_specs=(vmem, vmem, vmem, vmem),
        scratch_shapes=[
            pltpu.VMEM(queries.shape, jnp.bfloat16),
            pltpu.VMEM(text_kv.shape, jnp.bfloat16),
            pltpu.VMEM(visual_kv.shape, jnp.bfloat16),
            pltpu.VMEM((HEADS, HD), jnp.float32),
            pltpu.VMEM((32, HD), jnp.int32),
            pltpu.VMEM((32, HD), jnp.int32),
            pltpu.SMEM((2, HD), jnp.int32),
            pltpu.VMEM((24, HD), jnp.int32),
            pltpu.SMEM((24, HD), jnp.int32),
            pltpu.VMEM((SLOTS, BLOCK, HD), jnp.bfloat16),
            pltpu.VMEM((SLOTS, BLOCK, HD), jnp.bfloat16),
            pltpu.VMEM((4, VIS, HD), jnp.bfloat16),
            pltpu.VMEM((4, VIS, HD), jnp.bfloat16),
            pltpu.VMEM((4, 2 * VIS, HD), jnp.float32),
            pltpu.VMEM((SLOTS, 2 * TXT, HD), jnp.bfloat16),
            pltpu.VMEM((SLOTS, HD), jnp.float32),
            pltpu.VMEM((SLOTS, HD), jnp.float32),
            pltpu.VMEM((TENSOR, 1, HD), jnp.float32),
            pltpu.SemaphoreType.DMA((8,)),
            pltpu.SemaphoreType.DMA((SLOTS // CHUNK,)),
            pltpu.SemaphoreType.DMA((SLOTS // CHUNK,)),
            pltpu.SemaphoreType.DMA((1,)),
            pltpu.SemaphoreType.DMA((1,)),
            pltpu.SemaphoreType.DMA((1,)),
            pltpu.SemaphoreType.DMA((1,)),
            pltpu.SemaphoreType.DMA((TENSOR,)),
            pltpu.SemaphoreType.DMA((TENSOR,)),
        ],
        compiler_params=pltpu.CompilerParams(
            collective_id=0, has_side_effects=True, vmem_limit_bytes=60 * 1024 * 1024
        ),
        cost_estimate=pl.CostEstimate(flops=400_000_000, bytes_accessed=2_000_000, transcendentals=300_000),
    )(
        queries,
        text_kv,
        visual_kv,
        loss_gain.reshape(HEADS, HD),
        response_image.reshape(32, HD),
        visual_rows.reshape(2, HD),
        text_length.reshape(32, HD),
    )
    return pl.pallas_call(
        finish,
        out_shape=(
            jax.ShapeDtypeStruct(visual_kv.shape, jnp.bfloat16),
            jax.ShapeDtypeStruct(text_kv.shape, jnp.bfloat16),
            jax.ShapeDtypeStruct((N_DP,), jnp.float32),
        ),
        in_specs=[pl.BlockSpec(memory_space=pltpu.SMEM), vmem, vmem, vmem],
        out_specs=(vmem, vmem, vmem),
    )(owner, vis, back, loss)


def solution(mesh):
    in_specs = (
        P("dp", None, "tensor"),
        P("dp", None, "tensor"),
        P("dp", None, "tensor"),
        P("tensor"),
        P(),
        P(),
        P(),
    )
    out_specs = (P("dp", None, "tensor"), P("dp", None, "tensor"), P("dp"))
    return jax.shard_map(local, mesh=mesh, in_specs=in_specs, out_specs=out_specs, check_vma=False)
```

```python
import functools

import jax
import jax.numpy as jnp
from jax import lax
from jax.experimental import pallas as pl
from jax.experimental.pallas import tpu as pltpu
from jax.sharding import PartitionSpec as P

HD = 128
MESH = pl.DeviceIdType.MESH
SIDE = 8
N_DP = 64
TENSOR = 8
VIS = 64
TXT = 8
HEADS = 8
ROWS = HEADS * TXT
BLOCK = ROWS + 2 * TXT
KEYS = VIS + 2 * TXT
CHUNK = 4
SLOTS = N_DP
SELF = 3
SCALE = HD ** (-0.5)

NT = (((1,), (1,)), ((), ()))
NN = (((1,), (0,)), ((), ()))
TN = (((0,), (0,)), ((), ()))


def dot(left, right, dims):
    return lax.dot_general(left, right, dims, preferred_element_type=jnp.float32)


def turned(a, b):
    return ((a, b), (-a, -b), (b, -a), (-b, a))


TABLE = (((4, 4), (4, 0), (0, 4), (0, 0)),) + tuple(turned(*ab) for ab in ((4, 3), (1, 0), (4, 2), (1, 1), (3, 3), (2, 0), (4, 1), (1, 2), (2, 3), (2, 1), (3, 2), (3, 0), (1, 3), (3, 1), (2, 2)))


def offset(group, turn):
    return TABLE[group][turn]


def kernel(
    queries, text_kv, visual_kv, gain, images, rows_of, lengths,
    vis_out, back_recv, loss_out, owner_out,
    q_ref, text_ref, kv_ref, gain_ref, image_ref, length_ref, rows, meta_vec, meta,
    send_buf, recv_buf, key4, val4, acc, back_send, loss_send, loss_recv, loss_parts,
    load_sem, send_sem, recv_sem, back_send_sem, back_recv_sem, loss_send_sem, loss_recv_sem, part_send_sem, part_recv_sem,
):
    me = lax.axis_index("dp")
    core = lax.axis_index("tensor")
    z, y = lax.div(me, SIDE), lax.rem(me, SIDE)

    ahead_z = [lax.rem(z + step, SIDE) for step in range(SIDE)]
    ahead_y = [lax.rem(y + step, SIDE) for step in range(SIDE)]

    def target(group, turn):
        dz, dy = offset(group, turn)
        return ahead_z[dz % SIDE] * SIDE + ahead_y[dy % SIDE]

    def origin(group, turn):
        dz, dy = offset(group, turn)
        return lax.rem(z - dz + SIDE, SIDE), lax.rem(y - dy + SIDE, SIDE)

    pairs = [
        (images, image_ref), (lengths, length_ref), (rows_of, rows), (queries, q_ref), (text_kv, text_ref),
        (visual_kv, kv_ref), (gain, gain_ref),
    ]
    loads = [pltpu.make_async_copy(src, dst, load_sem.at[n]) for n, (src, dst) in enumerate(pairs)]
    for load in loads:
        load.start()

    barrier = pltpu.get_barrier_semaphore()

    def greet(step, carry):
        peer = lax.rem(me + step, N_DP)
        pl.semaphore_signal(barrier, inc=1, device_id=(peer, core), device_id_type=MESH)
        return carry

    lax.fori_loop(1, N_DP, greet, 0)
    for step in range(1, TENSOR):
        pl.semaphore_signal(barrier, inc=1, device_id=(me, (core + step) % TENSOR), device_id_type=MESH)

    loads[0].wait()
    loads[1].wait()
    half = me % 2
    lane128 = lax.broadcasted_iota(jnp.int32, (HD, HD), 1)
    row128 = lax.broadcasted_iota(jnp.int32, (HD, HD), 0)
    owner_row = image_ref[pl.ds(me // 2, 1)] // 4
    own_lane = lane128 // N_DP == half
    chosen = (owner_row == row128) & own_lane
    index8 = (lax.broadcasted_iota(jnp.int32, (8, HD), 1) - N_DP * half).astype(jnp.float32).astype(jnp.bfloat16)
    response_of = dot(index8, chosen.astype(jnp.float32).astype(jnp.bfloat16), NT)
    image_table = image_ref[...]
    held = image_table // 4 == me
    local_image = image_table % 4
    code = jnp.where(held, local_image + 4 * length_ref[...], 0).astype(jnp.float32)
    loads[2].wait()
    first_row, first_col = lax.div(4 * me, HD), lax.rem(4 * me, HD)
    seen = jnp.zeros_like(image_table)
    for image in range(4):
        seen = jnp.where(local_image == image, rows[first_row, first_col + image], seen)
    seen = jnp.where(held, seen, 0).astype(jnp.float32)
    code = jnp.concatenate([code, seen, jnp.zeros((HD - 64, HD), jnp.float32)], axis=0).astype(jnp.bfloat16)
    part = lax.broadcasted_iota(jnp.int32, (8, HD), 1) // N_DP == lax.broadcasted_iota(jnp.int32, (8, HD), 0)
    codes = dot(part.astype(jnp.float32).astype(jnp.bfloat16), code, NT)
    meta_vec[0:8] = jnp.clip(response_of.astype(jnp.int32), 0, N_DP - 1)
    meta_vec[8:16] = jnp.clip(codes.astype(jnp.int32), 0, HD - 1)
    meta_vec[16:24] = jnp.broadcast_to(owner_row, (8, HD))
    owner_out[...] = jnp.where(half == 0, owner_row, pltpu.roll(owner_row, N_DP, 1))
    to_scalars = pltpu.make_async_copy(meta_vec, meta, load_sem.at[7])
    to_scalars.start()
    loads[3].wait()
    loads[4].wait()
    to_scalars.wait()

    def stage(slot, peer, where):
        response = jnp.clip(meta[0, peer], 0, N_DP - 1)
        wide = q_ref[response].astype(jnp.float32)
        stacked = jnp.concatenate([wide[:, h * HD : (h + 1) * HD] for h in range(HEADS)], axis=0)
        where[slot, 0:ROWS] = stacked.astype(jnp.bfloat16)
        text = text_ref[response].astype(jnp.float32)
        pair = jnp.concatenate([text[:, 0:HD], text[:, HD : 2 * HD]], axis=0)
        where[slot, ROWS:BLOCK] = pair.astype(jnp.bfloat16)

    def send(slot, peer):
        pltpu.make_async_remote_copy(
            src_ref=send_buf.at[slot],
            dst_ref=recv_buf.at[slot],
            send_sem=send_sem.at[slot // CHUNK],
            recv_sem=recv_sem.at[slot // CHUNK],
            device_id=(peer, core),
            device_id_type=MESH,
        ).start()

    pl.semaphore_wait(barrier, N_DP - 1 + TENSOR - 1)

    for slot in range(SLOTS):
        if slot == 3:
            stage(slot, me, recv_buf)
        else:
            peer = target(slot // CHUNK, slot % CHUNK)
            stage(slot, peer, send_buf)
            send(slot, peer)

    for load in loads[5:]:
        load.wait()
    for image in range(4):
        key4[image] = kv_ref[image, :, 0:HD]
        val4[image] = kv_ref[image, :, HD : 2 * HD]
    acc[...] = jnp.zeros_like(acc)
    per_row = jnp.concatenate([jnp.broadcast_to(gain_ref[h : h + 1], (TXT, HD)) for h in range(HEADS)] * 2, axis=0)
    gain_t = per_row.T

    lane = lax.broadcasted_iota(jnp.int32, (1, HD), 1)
    first = lane < ROWS
    step_of = lane % TXT
    row = lax.broadcasted_iota(jnp.int32, (VIS + TXT, HD), 0)

    def key_rows(both):
        return jnp.where(first, both[0 : VIS + TXT], both[KEYS : KEYS + VIS + TXT])

    def value_rows(both):
        both = [jnp.concatenate([both[b : b + VIS], both[b + VIS + TXT : b + KEYS]], axis=0) for b in (0, KEYS)]
        return jnp.where(first, both[0], both[1])

    none = jnp.zeros((TXT, HD), jnp.float32)

    def diagonal(parts):
        values = jnp.concatenate(parts, axis=0)
        zero = jnp.zeros_like(values)
        return jnp.concatenate([jnp.where(first, values, zero), jnp.where(first, zero, values)], axis=0).astype(
            jnp.bfloat16
        )

    def work(group):
        pairs = []
        for half_of in range(2):
            slot = 4 * group + 2 * half_of
            images, lengths, seen = [], [], []
            for i in range(2):
                from_z, from_y = origin(group, 2 * half_of + i)
                code_row, code_lane = 8 + lax.rem(from_y, 2), from_z * 4 + lax.div(from_y, 2)
                code = meta[code_row, code_lane]
                images.append(jnp.clip(lax.rem(code, 4), 0, 3))
                lengths.append(lax.div(code, 4))
                seen.append(meta[code_row, 32 + code_lane])
            blocks = [recv_buf[slot + i] for i in range(2)]
            texts = [block[ROWS:BLOCK] for block in blocks]
            queries = jnp.concatenate([block[0:ROWS] for block in blocks], axis=0)
            keys = jnp.concatenate([key4[images[0]], texts[0], key4[images[1]], texts[1]], axis=0)
            values = jnp.concatenate([val4[images[0]], texts[0], val4[images[1]], texts[1]], axis=0)
            length = jnp.where(first, lengths[0], lengths[1])
            visible = jnp.where(first, seen[0], seen[1])
            pairs.append((images, queries, keys, values, length, visible))
        scores = [dot(keys, queries, NT) for _, queries, keys, _, _, _ in pairs]
        probs = []
        for (_, _, _, _, length, visible), score in zip(pairs, scores):
            text_end = VIS + jnp.minimum(step_of + 1, length)
            allowed = (row < visible) | ((row >= VIS) & (row < text_end))
            score = jnp.where(allowed, key_rows(score) * SCALE, jnp.float32(-1e30))
            raw = jnp.exp(score - jnp.max(score, axis=0, keepdims=True))
            probs.append(raw * (1.0 / jnp.sum(raw, axis=0, keepdims=True)))
        probs2 = [diagonal([prob[0:VIS], none, prob[VIS:]]) for prob in probs]
        attended = [dot(pair[3], prob2, TN) for pair, prob2 in zip(pairs, probs2)]
        cots, deltas, losses = [], [], []
        for pair, out in zip(pairs, attended):
            live = (step_of < pair[4]).astype(jnp.float32)
            weighted = gain_t * out * live
            loss_row = jnp.sum(weighted * out, axis=0, keepdims=True) * (1.0 / (2.0 * TXT * HD))
            cot = weighted.astype(jnp.bfloat16)
            cots.append(cot)
            deltas.append(jnp.sum(cot.astype(jnp.float32) * out, axis=0, keepdims=True))
            zero = jnp.zeros_like(loss_row)
            losses += [jnp.where(first, loss_row, zero), jnp.where(first, zero, loss_row)]
        prob_grads = [dot(pair[3], cot, NN) for pair, cot in zip(pairs, cots)]
        value_grads = [dot(prob2, cot, NT) for prob2, cot in zip(probs2, cots)]
        key_grads = []
        for pair, prob, grad, delta in zip(pairs, probs, prob_grads, deltas):
            score_grad2 = diagonal([prob * (value_rows(grad) - delta), none])
            key_grads.append(dot(score_grad2, pair[1], NN) * SCALE)
        images, backs, visuals = [], [], []
        for pair, key_grad, value_grad in zip(pairs, key_grads, value_grads):
            images += pair[0]
            for base in (0, KEYS):
                text_grad = [key_grad[base + VIS : base + VIS + TXT], value_grad[base + VIS + TXT : base + KEYS]]
                backs.append(jnp.concatenate(text_grad, axis=0).astype(jnp.bfloat16))
                visual = [key_grad[base : base + VIS], value_grad[base : base + VIS]]
                visuals.append(jnp.concatenate(visual, axis=0).astype(jnp.bfloat16).astype(jnp.float32))
        for image in range(4):
            total = acc[image]
            for held_image, visual in zip(images, visuals):
                total = total + jnp.where(held_image == image, visual, 0.0)
            acc[image] = total
        return backs, losses

    def back(slot, peer):
        pltpu.make_async_remote_copy(
            src_ref=back_send.at[slot],
            dst_ref=back_recv.at[me],
            send_sem=back_send_sem.at[0],
            recv_sem=back_recv_sem.at[0],
            device_id=(peer, core),
            device_id_type=MESH,
        ).start()

    def back_loss(slot, peer):
        pltpu.make_async_remote_copy(
            src_ref=loss_send.at[pl.ds(slot, 1)],
            dst_ref=loss_recv.at[pl.ds(me, 1)],
            send_sem=loss_send_sem.at[0],
            recv_sem=loss_recv_sem.at[0],
            device_id=(peer, core),
            device_id_type=MESH,
        ).start()

    def arrived(first_slot, count, chunk):
        pltpu.make_async_remote_copy(
            src_ref=send_buf.at[pl.ds(first_slot, count)],
            dst_ref=recv_buf.at[pl.ds(first_slot, count)],
            send_sem=send_sem.at[chunk],
            recv_sem=recv_sem.at[chunk],
            device_id=(me, core),
            device_id_type=MESH,
        ).wait_recv()

    def give_back(group):
        for turn in range(CHUNK if group else SELF):
            from_z, from_y = origin(group, turn)
            back(4 * group + turn, from_z * SIDE + from_y)

    for group in range(16):
        count = CHUNK if group else SELF
        arrived(4 * group, count, group)
        backs, losses = work(group)
        for turn in range(count):
            back_send[4 * group + turn] = backs[turn]
            loss_send[pl.ds(4 * group + turn, 1)] = losses[turn]
        if group == 0:
            back_recv[me] = backs[SELF]
            loss_recv[pl.ds(me, 1)] = losses[SELF]
        for turn in range(count):
            from_z, from_y = origin(group, turn)
            back_loss(4 * group + turn, from_z * SIDE + from_y)
    for group in sorted(range(16), key=lambda group: -sum(abs(step) for step in TABLE[group][0])):
        give_back(group)

    for image in range(4):
        total = acc[image]
        vis_out[image] = jnp.concatenate([total[0:VIS], total[VIS : 2 * VIS]], axis=1).astype(jnp.bfloat16)

    remote = SLOTS - 1
    losses_in = pltpu.make_async_remote_copy(
        src_ref=loss_send.at[pl.ds(0, remote)],
        dst_ref=loss_recv.at[pl.ds(0, remote)],
        send_sem=loss_send_sem.at[0],
        recv_sem=loss_recv_sem.at[0],
        device_id=(me, core),
        device_id_type=MESH,
    )
    losses_in.wait_recv()
    per_slot = jnp.sum(loss_recv[...], axis=1, keepdims=True)
    slot_id = lax.broadcasted_iota(jnp.int32, (SLOTS, HD), 0)
    mine = jnp.sum(jnp.where(slot_id == owner_row, per_slot, 0.0), axis=0, keepdims=True)
    loss_parts[core] = mine
    for step in range(1, TENSOR):
        pltpu.make_async_remote_copy(
            src_ref=loss_parts.at[core],
            dst_ref=loss_parts.at[core],
            send_sem=part_send_sem.at[step],
            recv_sem=part_recv_sem.at[step],
            device_id=(me, (core + step) % TENSOR),
            device_id_type=MESH,
        ).start()

    backs_in = pltpu.make_async_remote_copy(
        src_ref=back_send.at[pl.ds(0, remote)],
        dst_ref=back_recv.at[pl.ds(0, remote)],
        send_sem=back_send_sem.at[0],
        recv_sem=back_recv_sem.at[0],
        device_id=(me, core),
        device_id_type=MESH,
    )
    backs_in.wait_recv()

    total = mine
    for step in range(1, TENSOR):
        peer = (core + TENSOR - step) % TENSOR
        pltpu.make_async_remote_copy(
            src_ref=loss_parts.at[peer],
            dst_ref=loss_parts.at[peer],
            send_sem=part_send_sem.at[step],
            recv_sem=part_recv_sem.at[step],
            device_id=(me, core),
            device_id_type=MESH,
        ).wait()
        total = total + loss_parts[peer]
    loss_out[...] = jnp.where(half == 0, total, pltpu.roll(total, N_DP, 1))

    losses_in.wait_send()
    backs_in.wait_send()
    for chunk in range(SLOTS // CHUNK):
        count = CHUNK if chunk != 0 else 3
        pltpu.make_async_remote_copy(
            src_ref=send_buf.at[pl.ds(chunk * CHUNK, count)],
            dst_ref=recv_buf.at[pl.ds(chunk * CHUNK, count)],
            send_sem=send_sem.at[chunk],
            recv_sem=recv_sem.at[chunk],
            device_id=(me, core),
            device_id_type=MESH,
        ).wait_send()


def finish(owner, vis, back, loss, vis_out, text_out, loss_out):
    def place(response, carry):
        block = back[owner[0, response]].astype(jnp.float32)
        text_out[response] = jnp.concatenate([block[0:TXT], block[TXT : 2 * TXT]], axis=1).astype(jnp.bfloat16)
        return carry

    lax.fori_loop(0, N_DP, place, 0, unroll=8)
    vis_out[...] = vis[...]
    loss_out[...] = loss[0, 0:N_DP]


def local(queries, text_kv, visual_kv, loss_gain, response_image, visual_rows, text_length):
    vmem = pl.BlockSpec(memory_space=pltpu.VMEM)
    vis, back, loss, owner = pl.pallas_call(
        kernel,
        out_shape=(
            jax.ShapeDtypeStruct(visual_kv.shape, jnp.bfloat16),
            jax.ShapeDtypeStruct((SLOTS, 2 * TXT, HD), jnp.bfloat16),
            jax.ShapeDtypeStruct((1, HD), jnp.float32),
            jax.ShapeDtypeStruct((1, HD), jnp.int32),
        ),
        in_specs=[pl.BlockSpec(memory_space=pltpu.HBM)] * 7,
        out_specs=(vmem, vmem, vmem, vmem),
        scratch_shapes=[
            pltpu.VMEM(queries.shape, jnp.bfloat16),
            pltpu.VMEM(text_kv.shape, jnp.bfloat16),
            pltpu.VMEM(visual_kv.shape, jnp.bfloat16),
            pltpu.VMEM((HEADS, HD), jnp.float32),
            pltpu.VMEM((32, HD), jnp.int32),
            pltpu.VMEM((32, HD), jnp.int32),
            pltpu.SMEM((2, HD), jnp.int32),
            pltpu.VMEM((24, HD), jnp.int32),
            pltpu.SMEM((24, HD), jnp.int32),
            pltpu.VMEM((SLOTS, BLOCK, HD), jnp.bfloat16),
            pltpu.VMEM((SLOTS, BLOCK, HD), jnp.bfloat16),
            pltpu.VMEM((4, VIS, HD), jnp.bfloat16),
            pltpu.VMEM((4, VIS, HD), jnp.bfloat16),
            pltpu.VMEM((4, 2 * VIS, HD), jnp.float32),
            pltpu.VMEM((SLOTS, 2 * TXT, HD), jnp.bfloat16),
            pltpu.VMEM((SLOTS, HD), jnp.float32),
            pltpu.VMEM((SLOTS, HD), jnp.float32),
            pltpu.VMEM((TENSOR, 1, HD), jnp.float32),
            pltpu.SemaphoreType.DMA((8,)),
            pltpu.SemaphoreType.DMA((SLOTS // CHUNK,)),
            pltpu.SemaphoreType.DMA((SLOTS // CHUNK,)),
            pltpu.SemaphoreType.DMA((1,)),
            pltpu.SemaphoreType.DMA((1,)),
            pltpu.SemaphoreType.DMA((1,)),
            pltpu.SemaphoreType.DMA((1,)),
            pltpu.SemaphoreType.DMA((TENSOR,)),
            pltpu.SemaphoreType.DMA((TENSOR,)),
        ],
        compiler_params=pltpu.CompilerParams(
            collective_id=0, has_side_effects=True, vmem_limit_bytes=60 * 1024 * 1024
        ),
        cost_estimate=pl.CostEstimate(flops=400_000_000, bytes_accessed=2_000_000, transcendentals=300_000),
    )(
        queries,
        text_kv,
        visual_kv,
        loss_gain.reshape(HEADS, HD),
        response_image.reshape(32, HD),
        visual_rows.reshape(2, HD),
        text_length.reshape(32, HD),
    )
    return pl.pallas_call(
        finish,
        out_shape=(
            jax.ShapeDtypeStruct(visual_kv.shape, jnp.bfloat16),
            jax.ShapeDtypeStruct(text_kv.shape, jnp.bfloat16),
            jax.ShapeDtypeStruct((N_DP,), jnp.float32),
        ),
        in_specs=[pl.BlockSpec(memory_space=pltpu.SMEM), vmem, vmem, vmem],
        out_specs=(vmem, vmem, vmem),
    )(owner, vis, back, loss)


def solution(mesh):
    in_specs = (
        P("dp", None, "tensor"),
        P("dp", None, "tensor"),
        P("dp", None, "tensor"),
        P("tensor"),
        P(),
        P(),
        P(),
    )
    out_specs = (P("dp", None, "tensor"), P("dp", None, "tensor"), P("dp"))
    return jax.shard_map(local, mesh=mesh, in_specs=in_specs, out_specs=out_specs, check_vma=False)
```
